256 devices in a mesh: segment: 8 (over z_hi, x), dp: 32 (over z_lo, y, core).
Axes of the slice: x: 4, y: 4, z: 8 (z_hi: 2, z_lo: 4; z = z_hi * 4 + z_lo), core: 2. Of those that a mesh axis runs over, the one named last changes fastest.
Arguments:
- fine_inflow: bfloat16 [8, 32, 16, 16, 256], P('segment', 'dp'), may hold values from -250 to 250
- coarse_inflow: bfloat16 [8, 32, 8, 8, 512], P('segment', 'dp'), may hold values from -250 to 250
- fine_entries: bfloat16 [3, 32, 16, 16, 256], P(None, 'dp'), may hold values from -250 to 250
- fine_pending: bfloat16 [8, 6, 32, 16, 16, 256], P('segment', None, 'dp'), may hold values from -250 to 250, as said below
- coarse_pending: bfloat16 [8, 2, 32, 8, 8, 512], P('segment', None, 'dp'), may hold values from -250 to 250, as said below
- fine_kernels: bfloat16 [8, 2, 3, 3, 256, 256], P('segment'), may hold values from -0.125 to 0.125
- fine_mixing: bfloat16 [8, 256, 256], P('segment'), may hold values from -0.375 to 0.375
- fine_gains: float32 [8, 2, 256], P('segment'), may hold values from 0.5 to 1.5
- fine_shifts: float32 [8, 2, 256], P('segment'), may hold values from -3 to 3
- coarse_kernel: bfloat16 [8, 3, 3, 512, 512], P('segment'), may hold values from -0.09375 to 0.09375
- coarse_mixing: bfloat16 [8, 512, 512], P('segment'), may hold values from -0.25 to 0.25
- coarse_gains: float32 [8, 512], P('segment'), may hold values from 0.5 to 1.5
- coarse_shifts: float32 [8, 512], P('segment'), may hold values from -3 to 3
- descent_kernel: bfloat16 [2, 2, 256, 512], replicated, may hold values from -0.1875 to 0.1875
- upsample_kernel: bfloat16 [512, 2, 2, 256], replicated, may hold values from -0.25 to 0.25
Outputs:
- fine_stash: bfloat16 [8, 4, 32, 16, 16, 256], P('segment', None, 'dp')
- coarse_stash: bfloat16 [8, 4, 32, 8, 8, 512], P('segment', None, 'dp')
- fine_backlog: bfloat16 [8, 6, 32, 16, 16, 256], P('segment', None, 'dp')
- coarse_backlog: bfloat16 [8, 2, 32, 8, 8, 512], P('segment', None, 'dp')
The draws below stay inside these ranges and needn't reach their ends.
Inputs may be any that keep to these rules, and one draw needn't show every extreme that they name: `fine_pending`: at segments 4 and above only the first 6 slots are read. `coarse_pending`: at segments below 4 only the first 2 slots are read.
All inputs are finite; a program needn't handle non-finite values.
Results may differ from the reference program's by a relative error of at most 0.017.
Values may be sent and summed in bfloat16 or wider, within the bound.
No kernel may reach another device: no remote copies, remote signals or barrier semaphores. Data moves between devices by JAX's collectives and lax.ppermute only.
A program may use at most 64 MiB of HBM per device.

```python
import jax
import jax.numpy as jnp
from jax import lax

FINE_CH = 256
COARSE_CH = 512
TILE = 16
TICKS = 4
CTILE = 8
HOLD_FINE = 6
RECV_FINE = 6
HOLD_COARSE = 2
RECV_COARSE = 2
N_SEGMENT = 8
N_DP = 32


def spread_tiles(key, tile_shape, dp_dim):
    base_key, rows_key, cols_key = jax.random.split(key, 3)
    normal_part = jnp.clip(jax.random.normal(base_key, tile_shape, jnp.float32), -6.0, 6.0)
    dp_place = lax.broadcasted_iota(jnp.float32, tile_shape, dp_dim)
    rising = 0.4 * jnp.exp(jnp.log(6.0) * dp_place / (N_DP - 1))
    row_scale = jnp.exp(jax.random.uniform(rows_key, tile_shape[:-1] + (1,), jnp.float32, jnp.log(0.3), jnp.log(3.0)))
    columns = jnp.exp(jax.random.uniform(cols_key, (tile_shape[-1],), jnp.float32, jnp.log(0.5), jnp.log(5.0)))
    return (normal_part * rising * row_scale * columns).astype(jnp.bfloat16)


def draw_fine_inflow(key, part):
    return spread_tiles(jax.random.fold_in(key, 11), (N_SEGMENT, N_DP, TILE, TILE, FINE_CH), 1)


def draw_coarse_inflow(key, part):
    return spread_tiles(jax.random.fold_in(key, 12), (N_SEGMENT, N_DP, CTILE, CTILE, COARSE_CH), 1)


def draw_fine_entries(key, part):
    return spread_tiles(jax.random.fold_in(key, 13), (TICKS - 1, N_DP, TILE, TILE, FINE_CH), 1)


def draw_fine_pending(key, part):
    return spread_tiles(jax.random.fold_in(key, 14), (N_SEGMENT, HOLD_FINE, N_DP, TILE, TILE, FINE_CH), 2)


def draw_coarse_pending(key, part):
    return spread_tiles(jax.random.fold_in(key, 15), (N_SEGMENT, HOLD_COARSE, N_DP, CTILE, CTILE, COARSE_CH), 2)


def block_scale(stream_key, shape, cuts, low, top_value):
    level, own = 1.0, jax.random.fold_in(stream_key, 6)
    for dim, parts in cuts:
        draws = jnp.exp(jax.random.uniform(jax.random.fold_in(own, dim), (parts,), jnp.float32, low / len(cuts), top_value / len(cuts)))
        level = level * jnp.repeat(draws, shape[dim] // parts).reshape([-1 if axis == dim else 1 for axis in range(len(shape))])
    return level


def bell_draw(key, extent, width, bound, pieces=(), kind=jnp.bfloat16):
    loudness = block_scale(key, extent, pieces, -0.22, 0.18) if pieces else 1.0
    array = jax.random.normal(key, extent, jnp.float32) * width * loudness
    return jnp.minimum(jnp.maximum(array, -bound), bound).astype(kind)


def setup_inputs(seed: int = 0) -> dict:
    seeds = jax.random.split(jax.random.key(seed), 16)
    return {
        "fine_inflow": draw_fine_inflow(jax.random.fold_in(seeds[15], 71), 0),
        "coarse_inflow": draw_coarse_inflow(jax.random.fold_in(seeds[15], 71), 0),
        "fine_entries": draw_fine_entries(jax.random.fold_in(seeds[15], 71), 0),
        "fine_pending": draw_fine_pending(jax.random.fold_in(seeds[15], 71), 0),
        "coarse_pending": draw_coarse_pending(jax.random.fold_in(seeds[15], 71), 0),
        "fine_kernels": bell_draw(seeds[5], (N_SEGMENT, 2, 3, 3, FINE_CH, FINE_CH), (9 * FINE_CH) ** -0.5, 0.125, ((0, 8),)),
        "fine_mixing": bell_draw(seeds[6], (N_SEGMENT, FINE_CH, FINE_CH), FINE_CH ** -0.5, 0.375, ((0, 8),)),
        "fine_gains": jnp.clip(0.5 + 1.0 * jax.random.uniform(seeds[7], (N_SEGMENT, 2, FINE_CH), jnp.float32) ** block_scale(seeds[7], (N_SEGMENT, 2, FINE_CH), ((0, 8),), -0.2, 0.2), 0.5, 1.5),
        "fine_shifts": bell_draw(seeds[8], (N_SEGMENT, 2, FINE_CH), 0.5, 3.0, ((0, 8),), jnp.float32),
        "coarse_kernel": bell_draw(seeds[9], (N_SEGMENT, 3, 3, COARSE_CH, COARSE_CH), (9 * COARSE_CH) ** -0.5, 0.09375, ((0, 8),)),
        "coarse_mixing": bell_draw(seeds[10], (N_SEGMENT, COARSE_CH, COARSE_CH), COARSE_CH ** -0.5, 0.25, ((0, 8),)),
        "coarse_gains": jnp.clip(0.5 + 1.0 * jax.random.uniform(seeds[11], (N_SEGMENT, COARSE_CH), jnp.float32) ** block_scale(seeds[11], (N_SEGMENT, COARSE_CH), ((0, 8),), -0.2, 0.2), 0.5, 1.5),
        "coarse_shifts": bell_draw(seeds[12], (N_SEGMENT, COARSE_CH), 0.5, 3.0, ((0, 8),), jnp.float32),
        "descent_kernel": bell_draw(seeds[13], (2, 2, FINE_CH, COARSE_CH), (4 * FINE_CH) ** -0.5, 0.1875),
        "upsample_kernel": bell_draw(seeds[14], (COARSE_CH, 2, 2, FINE_CH), COARSE_CH ** -0.5, 0.25),
    }


EPSILON = 1e-05

def convolve(images, kernel):
    return lax.conv_general_dilated(images, kernel, (1, 1), 'SAME', dimension_numbers=('NHWC', 'HWIO', 'NHWC'), preferred_element_type=jnp.float32)

def project(images, matrix):
    flat = images.reshape(-1, images.shape[-1])
    result = jnp.dot(flat, matrix, preferred_element_type=jnp.float32)
    return result.reshape(images.shape[:-1] + (matrix.shape[1],))

def descend(images, kernel):
    lowered = lax.conv_general_dilated(images, kernel, (2, 2), 'VALID', dimension_numbers=('NHWC', 'HWIO', 'NHWC'), preferred_element_type=jnp.float32)
    return lowered.astype(jnp.bfloat16)

def upsample(images, kernel):
    batches, height, breadth, coarse = images.shape
    fine_ch = kernel.shape[-1]
    spread = project(images, kernel.reshape(coarse, 4 * fine_ch))
    spread = spread.reshape(batches, height, breadth, 2, 2, fine_ch).transpose(0, 1, 3, 2, 4, 5)
    return spread.reshape(batches, 2 * height, 2 * breadth, fine_ch).astype(jnp.bfloat16)

def activate(values, gain, shift):
    center = lax.optimization_barrier(jnp.mean(values, axis=(0, 1, 2)))
    spread = lax.optimization_barrier(jnp.mean(jnp.square(values - center), axis=(0, 1, 2)))
    scaled = (values - center) * lax.rsqrt(spread + EPSILON) * gain + shift
    return jnp.maximum(scaled, 0.0).astype(jnp.bfloat16)

def reference(fine_inflow, coarse_inflow, fine_entries, fine_pending, coarse_pending, fine_kernels, fine_mixing, fine_gains, fine_shifts, coarse_kernel, coarse_mixing, coarse_gains, coarse_shifts, descent_kernel, upsample_kernel):
    half_depth = N_SEGMENT // 2
    fine_now = [fine_inflow[position] for position in range(N_SEGMENT)]
    coarse_now = [coarse_inflow[position] for position in range(N_SEGMENT)]
    sender_fine = [[fine_pending[pair_index, slot_index] for slot_index in range(HOLD_FINE)] for pair_index in range(half_depth)]
    receiver_fine = [[fine_pending[pair_index + half_depth, slot_index] for slot_index in range(RECV_FINE)] for pair_index in range(half_depth)]
    sender_coarse = [[coarse_pending[pair_index + half_depth, slot_index] for slot_index in range(HOLD_COARSE)] for pair_index in range(half_depth)]
    receiver_coarse = [[coarse_pending[pair_index, slot_index] for slot_index in range(RECV_COARSE)] for pair_index in range(half_depth)]
    fine_store = [[] for position in range(N_SEGMENT)]
    coarse_store = [[] for position in range(N_SEGMENT)]
    for tick_now in range(TICKS):
        if tick_now > 0:
            fine_last = [fine_store[position][-1] for position in range(N_SEGMENT)]
            coarse_last = [coarse_store[position][-1] for position in range(N_SEGMENT)]
            shifted_fine = [fine_entries[tick_now - 1]] + fine_last[:-1]
            shifted_coarse = [coarse_last[-1]] + coarse_last[:-1]
            shifted_fine[half_depth] = upsample(coarse_last[half_depth - 1], upsample_kernel)
            shifted_coarse[half_depth] = descend(fine_last[half_depth - 1], descent_kernel)
            fine_now = shifted_fine
            coarse_now = shifted_coarse
        for pair_index in range(half_depth):
            receiver_fine[pair_index].append(sender_fine[pair_index][tick_now])
            receiver_coarse[pair_index].append(sender_coarse[pair_index][tick_now])
        for position in range(N_SEGMENT):
            if position < half_depth:
                fine_input = fine_now[position]
                coarse_taken = receiver_coarse[position][tick_now]
                coarse_input = (project(coarse_now[position], coarse_mixing[position]) + coarse_taken.astype(jnp.float32)).astype(jnp.bfloat16)
            else:
                fine_taken = receiver_fine[position - half_depth][tick_now]
                fine_input = (project(fine_now[position], fine_mixing[position]) + fine_taken.astype(jnp.float32)).astype(jnp.bfloat16)
                coarse_input = coarse_now[position]
            fine_first = activate(convolve(fine_input, fine_kernels[position, 0]), fine_gains[position, 0], fine_shifts[position, 0])
            fine_out = activate(convolve(fine_first, fine_kernels[position, 1]), fine_gains[position, 1], fine_shifts[position, 1])
            coarse_out = activate(convolve(coarse_input, coarse_kernel[position]), coarse_gains[position], coarse_shifts[position])
            fine_store[position].append(fine_out)
            coarse_store[position].append(coarse_out)
            if position < half_depth:
                sender_fine[position].append(project(fine_out, fine_mixing[position]).astype(jnp.bfloat16))
            else:
                sender_coarse[position - half_depth].append(project(coarse_out, coarse_mixing[position]).astype(jnp.bfloat16))
    fine_stash = jnp.stack([jnp.stack(fine_store[position]) for position in range(N_SEGMENT)])
    coarse_stash = jnp.stack([jnp.stack(coarse_store[position]) for position in range(N_SEGMENT)])
    fine_zero = jnp.zeros_like(fine_inflow[0])
    coarse_zero = jnp.zeros_like(coarse_inflow[0])
    fine_rows = []
    coarse_rows = []
    for position in range(N_SEGMENT):
        if position < half_depth:
            fine_rows.append(jnp.stack(sender_fine[position][TICKS:TICKS + HOLD_FINE]))
            chosen = receiver_coarse[position][TICKS:TICKS + RECV_COARSE] + [coarse_zero] * (HOLD_COARSE - RECV_COARSE)
            coarse_rows.append(jnp.stack(chosen))
        else:
            chosen = receiver_fine[position - half_depth][TICKS:TICKS + RECV_FINE] + [fine_zero] * (HOLD_FINE - RECV_FINE)
            fine_rows.append(jnp.stack(chosen))
            coarse_rows.append(jnp.stack(sender_coarse[position - half_depth][TICKS:TICKS + HOLD_COARSE]))
    return (fine_stash, coarse_stash, jnp.stack(fine_rows), jnp.stack(coarse_rows))
```

```python
import functools

import jax
import jax.numpy as jnp
from jax import lax
from jax.experimental import pallas as pl
from jax.experimental.pallas import tpu as pltpu
from jax.sharding import PartitionSpec as P

EPSILON = 1e-05
BF16 = jnp.bfloat16
F32 = jnp.float32
LIMIT = 24 * 1024 * 1024

SIDE, CSIDE = 16, 8
CELLS, CCELLS = SIDE * SIDE, CSIDE * CSIDE
FCH, CCH = 256, 512
N_DP = 32
HALF = 4
LAST = 2 * HALF - 1
TICKS = 4


def call(body, outs, in_specs, scratch=(), flops=0, moved=0, aliases=None):
    kernel = pl.pallas_call(
        body,
        out_shape=[space(*rest) if len(rest) == 2 else space(*rest, BF16) for space, *rest in outs],
        in_specs=in_specs,
        out_specs=[VM if space is pltpu.VMEM else ANY for space, *_ in outs],
        scratch_shapes=list(scratch),
        input_output_aliases=aliases or {},
        compiler_params=pltpu.CompilerParams(vmem_limit_bytes=LIMIT),
        cost_estimate=pl.CostEstimate(flops=flops, bytes_accessed=moved, transcendentals=0),
    )
    spaces = {id(VM): pltpu.VMEM, id(ANY): pltpu.HBM}

    def placed(spec, x):
        return pltpu.with_memory_space_constraint(x, spaces[id(spec)]) if id(spec) in spaces else x

    return lambda *args: kernel(*[placed(spec, arg) for spec, arg in zip(in_specs, args, strict=True)])


VM = pl.BlockSpec(memory_space=pltpu.VMEM)
SM = pl.BlockSpec(memory_space=pltpu.SMEM)
ANY = pl.BlockSpec(memory_space=pl.ANY)


def dot(a, b):
    return jnp.dot(a, b, preferred_element_type=F32)


def lanes(rows):
    return jnp.concatenate([rows[i : i + 1] for i in range(rows.shape[0])], axis=1)


def rows_of(line):
    return [line[:, i : i + 128] for i in range(0, line.shape[1], 128)]


def with_neighbours(x, width):
    count = x.shape[0]
    column = lax.broadcasted_iota(jnp.int32, x.shape, 0) & (width - 1)
    left = jnp.where(column == 0, 0.0, pltpu.roll(x, 1, 0))
    right = jnp.where(column == width - 1, 0.0, pltpu.roll(x, count - 1, 0))
    return left, x, right


class Streamed:
    def __init__(self, source, held, sems):
        self.held = held
        self.copies = [
            pltpu.make_async_copy(source.at[i], held.at[i], sems.at[i]) for i in range(held.shape[0])
        ]

    def start(self):
        for copy in self.copies:
            copy.start()
        return self

    def __getitem__(self, i):
        self.copies[i].wait()
        return self.held[i]


def fine_convolution(x, padded, kernel):
    edge = jnp.zeros((SIDE, 3 * FCH), BF16)
    padded[0:SIDE, :] = edge
    padded[SIDE + CELLS : 2 * SIDE + CELLS, :] = edge
    for i, piece in enumerate(with_neighbours(x, SIDE)):
        padded[SIDE : SIDE + CELLS, i * FCH : (i + 1) * FCH] = piece.astype(BF16)
    total = dot(padded[0:CELLS, :], kernel[0])
    total += dot(padded[SIDE : SIDE + CELLS, :], kernel[1])
    total += dot(padded[2 * SIDE : 2 * SIDE + CELLS, :], kernel[2])
    return total


def local_moments(h):
    mean = jnp.sum(h, axis=0, keepdims=True) * (1.0 / h.shape[0])
    away = h - mean
    return mean, jnp.sum(away * away, axis=0, keepdims=True)


def merged(pieces, cells_each):
    count = len(pieces)
    k = pieces[0].shape[0] // 2
    total = functools.reduce(jnp.add, pieces)
    mean = total * (1.0 / count)
    drift = functools.reduce(jnp.add, [jnp.square(piece - mean) for piece in pieces])
    spread = (total[k:] + cells_each * drift[:k]) * (1.0 / (count * cells_each))
    return lanes(mean[:k]), lanes(spread)


def activated(h, mean, spread, gain, shift):
    return jnp.maximum((h - mean) * lax.rsqrt(spread + EPSILON) * gain + shift, 0.0)


def fine_first(tick, *refs):
    if tick == 0:
        place, inflow, pending, mixing, kernels, cpending = refs[:6]
        refs = refs[6:]
    else:
        place, arrived, raised_in, entries, raising, pending, mixing, kernels = refs[:8]
        refs = refs[8:]
    h_ref, pay_ref = refs[:2]
    x_ref, padded, skip_ref, mix_ref, held, sems = refs[(3 if tick == 0 else 2) :][:6]
    segment = place[0]
    kernel = Streamed(kernels.at[0], held, sems.at[pl.ds(0, 3)])
    skip = pltpu.make_async_copy(pending.at[tick], skip_ref, sems.at[3])
    mix = pltpu.make_async_copy(mixing, mix_ref, sems.at[4])

    if tick == 0:
        x = pltpu.make_async_copy(inflow, x_ref, sems.at[5])
        x.start()
    else:
        spread_ref, up_ref, up_sems = refs[8:]
        up = Streamed(raising, up_ref, up_sems)

        @pl.when(segment == HALF)
        def _():
            up.start()

        @pl.when(segment == 0)
        def _():
            pltpu.make_async_copy(entries.at[tick - 1], x_ref, sems.at[5]).start()

    @pl.when(segment >= HALF)
    def _():
        mix.start()
        skip.start()

    kernel.start()
    if tick == 0:
        packed, staged, pack_sems = refs[2], refs[9], refs[10]
        loads = [pltpu.make_async_copy(pending.at[slot], staged.at[slot], pack_sems.at[slot]) for slot in range(4)]
        cloads = [
            pltpu.make_async_copy(
                cpending.at[slot, :, pl.ds(side * FCH, FCH)],
                staged.at[0, pl.ds((2 * slot + side) * CCELLS, CCELLS)],
                pack_sems.at[2 * slot + side],
            )
            for slot in range(2)
            for side in range(2)
        ]
        store = pltpu.make_async_copy(staged, packed, pack_sems.at[4])
        cstore = pltpu.make_async_copy(staged.at[0], packed.at[0], pack_sems.at[4])

        @pl.when(segment < HALF)
        def _():
            for copy in loads:
                copy.start()

        @pl.when(segment >= HALF)
        def _():
            for copy in cloads:
                copy.start()

    if tick == 0:
        x.wait()
    else:

        @pl.when(segment == 0)
        def _():
            pltpu.make_async_copy(entries.at[tick - 1], x_ref, sems.at[5]).wait()

        @pl.when((segment != 0) & (segment != HALF))
        def _():
            x_ref[...] = arrived[...]

        @pl.when(segment == HALF)
        def _():
            for part in range(4):
                raised = dot(raised_in[...], up[part])
                for i in range(CSIDE):
                    start = (2 * i + part // 2) * SIDE + part % 2
                    for p in range(FCH // 128):
                        spread_ref[p, pl.ds(start, CSIDE, stride=2), :] = raised[
                            i * CSIDE : (i + 1) * CSIDE, p * 128 : (p + 1) * 128
                        ]
            for p in range(FCH // 128):
                x_ref[:, p * 128 : (p + 1) * 128] = spread_ref[p].astype(BF16)

    @pl.when(segment >= HALF)
    def _():
        skip.wait()
        mix.wait()
        x_ref[...] = (dot(x_ref[...], mix_ref[...]) + skip_ref[...].astype(F32)).astype(BF16)

    if tick == 0:

        @pl.when(segment < HALF)
        def _():
            for copy in loads:
                copy.wait()
            store.start()

        @pl.when(segment >= HALF)
        def _():
            for copy in cloads:
                copy.wait()
            cstore.start()

    h = fine_convolution(x_ref[...].astype(F32), padded, kernel)
    h_ref[...] = h
    mean, spread = local_moments(h)
    pay = jnp.concatenate(rows_of(mean) + rows_of(spread), axis=0)
    pay_ref[...] = jnp.broadcast_to(pay[None], pay_ref.shape)
    if tick == 0:

        @pl.when(segment < HALF)
        def _():
            store.wait()

        @pl.when(segment >= HALF)
        def _():
            cstore.wait()


def coarse_first(tick, *refs):
    place, arrived, pending, mixing, kernels = refs[:5]
    h_ref, mine_ref, other_ref, x_ref, padded, mix_ref, held, sems, skip_ref = refs[5:]
    kernel = Streamed(kernels, held, sems.at[pl.ds(3, 3)])
    if tick < 2:
        skips = [pltpu.make_async_copy(pending.at[tick], skip_ref, sems.at[1])]
    else:
        skips = [
            pltpu.make_async_copy(
                pending.at[1, 0, pl.ds((2 * (tick - 2) + side) * CCELLS, CCELLS)],
                skip_ref.at[:, pl.ds(side * FCH, FCH)],
                sems.at[(1, 6)[side]],
            )
            for side in range(2)
        ]
    segment = place[0]
    mix = pltpu.make_async_copy(mixing, mix_ref, sems.at[0])

    @pl.when(segment < HALF)
    def _():
        mix.start()
        for skip in skips:
            skip.start()

    if tick == 0:
        fetch = pltpu.make_async_copy(arrived, x_ref, sems.at[2])
        fetch.start()
    kernel.start()
    if tick == 0:
        fetch.wait()
    else:
        x_ref[...] = arrived[...]
    @pl.when(segment < HALF)
    def _():
        mix.wait()
        for skip in skips:
            skip.wait()
        x_ref[...] = (dot(x_ref[...], mix_ref[...]) + skip_ref[...].astype(F32)).astype(BF16)

    edge = jnp.zeros((CSIDE, CCH), F32)
    for i, piece in enumerate(with_neighbours(x_ref[...].astype(F32), CSIDE)):
        columns = slice(i * CCH, (i + 1) * CCH)
        padded[0, :, columns] = jnp.concatenate([edge, piece[: CCELLS - CSIDE]], axis=0).astype(BF16)
        padded[1, :, columns] = piece.astype(BF16)
        padded[2, :, columns] = jnp.concatenate([piece[CSIDE:], edge], axis=0).astype(BF16)
    h = dot(padded[0], kernel[0])
    h += dot(padded[1], kernel[1])
    h += dot(padded[2], kernel[2])
    h_ref[...] = h
    mean, spread = local_moments(h)
    mean, spread = rows_of(mean), rows_of(spread)
    first = jnp.concatenate(mean[:2] + spread[:2], axis=0)
    second = jnp.concatenate(mean[2:] + spread[2:], axis=0)
    is_first = place[1] == 0
    mine_ref[...] = jnp.where(is_first, first, second)
    other_ref[...] = jnp.where(is_first, second, first)


def fine_second(gathered, h_ref, gains, shifts, kernels, mine, theirs, out_ref, pay_ref, padded, held, sems):
    kernel = Streamed(kernels.at[1], held, sems).start()
    mean, spread = merged([gathered[i] for i in range(N_DP)], float(CELLS))
    x = activated(h_ref[...], mean, spread, gains[0:1], shifts[0:1]).astype(BF16)
    h = fine_convolution(x.astype(F32), padded, kernel)
    out_ref[...] = h
    mean, spread = local_moments(h)
    a, b = mine[...], theirs[...]
    pair_mean = (a[:2] + b[:2]) * 0.5
    pair_spread = a[2:] + b[2:] + jnp.square(a[:2] - b[:2]) * (0.5 * CCELLS)
    pay = jnp.concatenate(rows_of(mean) + rows_of(spread) + [pair_mean, pair_spread], axis=0)
    pay_ref[...] = jnp.broadcast_to(pay[None], pay_ref.shape)


def finish(tick, place, gathered, h_ref, hc_ref, gains, shifts, cgains, cshifts, *refs):
    if tick == TICKS - 1:
        fine_ref, coarse_ref = refs
    else:
        descent, fine_ref, coarse_ref, going, fine32, packed, down_ref, sem = refs
        fetch = pltpu.make_async_copy(descent, down_ref, sem)

        @pl.when(place[0] == HALF - 1)
        def _():
            fetch.start()

    mean, spread = merged([gathered[i, 0:4] for i in range(N_DP)], float(CELLS))
    fine = activated(h_ref[...], mean, spread, gains[1:2], shifts[1:2]).astype(BF16)
    mean0, spread0 = merged([gathered[i, 4:8] for i in range(0, N_DP, 2)], 2.0 * CCELLS)
    mean1, spread1 = merged([gathered[i, 4:8] for i in range(1, N_DP, 2)], 2.0 * CCELLS)
    mean = jnp.concatenate([mean0, mean1], axis=1)
    spread = jnp.concatenate([spread0, spread1], axis=1)
    coarse = activated(hc_ref[...], mean, spread, cgains[...], cshifts[...]).astype(BF16)
    fine_ref[...] = fine
    coarse_ref[...] = coarse
    if tick < TICKS - 1:
        segment = place[0]

        @pl.when(segment != HALF - 1)
        def _():
            going[...] = coarse

        @pl.when(segment == HALF - 1)
        def _():
            for p in range(FCH // 128):
                fine32[...] = fine[:, p * 128 : (p + 1) * 128].astype(F32)
                for a in range(2):
                    for c in range(2):
                        taken = [
                            fine32[pl.ds((2 * i + a) * SIDE + c, CSIDE, stride=2), :] for i in range(CSIDE)
                        ]
                        column = (2 * a + c) * FCH + p * 128
                        packed[:, column : column + 128] = jnp.concatenate(taken, axis=0).astype(BF16)
            fetch.wait()
            going[...] = dot(packed[...], down_ref[...]).astype(BF16)


def keep(tick, *refs):
    place, fine, coarse, mixing, cmixing = refs[:5]
    refs = refs[5:]
    if tick != 1:
        extra, refs = refs[0], refs[1:]
    fstash, cstash, fback, ctarget, term, cterm, mix_ref, cmix_ref, staged, sems = refs[(0, 4, 3, 4)[tick] :]
    segment = place[0]
    copies = [
        pltpu.make_async_copy(fine, fstash.at[tick], sems.at[0]),
        pltpu.make_async_copy(coarse, cstash.at[tick], sems.at[1]),
    ]
    for copy in copies:
        copy.start()
    if tick == 0:
        load = pltpu.make_async_copy(extra.at[4:6], staged.at[0:2], sems.at[2])
        load.start()

    @pl.when(segment < HALF)
    def _():
        fetch = pltpu.make_async_copy(mixing, mix_ref, sems.at[3])
        fetch.start()
        if tick == 3:
            ccopy = pltpu.make_async_copy(extra, ctarget, sems.at[5])
            ccopy.start()
        fetch.wait()
        term[...] = dot(fine[...], mix_ref[...]).astype(BF16)
        copy = pltpu.make_async_copy(term, fback.at[2 + tick], sems.at[4])
        copy.start()
        if tick == 3:
            ccopy.wait()
        copy.wait()

    @pl.when(segment >= HALF)
    def _():
        fetch = pltpu.make_async_copy(cmixing, cmix_ref, sems.at[3])
        fetch.start()
        if tick == 2:
            received = pltpu.make_async_copy(extra.at[0], staged, sems.at[4])
            received.start()
        fetch.wait()
        cterm[...] = dot(coarse[...], cmix_ref[...]).astype(BF16)
        copy = pltpu.make_async_copy(cterm, ctarget.at[tick % 2], sems.at[5])
        copy.start()
        if tick == 2:
            received.wait()
            stored = pltpu.make_async_copy(staged, fback.at[2:6], sems.at[4])
            stored.start()
            stored.wait()
        copy.wait()

    if tick == 0:
        load.wait()
        store = pltpu.make_async_copy(staged.at[0:2], fback.at[0:2], sems.at[2])
        store.start()
        store.wait()
    for copy in copies:
        copy.wait()


def kept_after(tick, common, added, kept):
    stashes = [
        (pltpu.HBM, (TICKS, CELLS, FCH)),
        (pltpu.HBM, (TICKS, CCELLS, CCH)),
        (pltpu.HBM, (6, CELLS, FCH)),
        (pltpu.HBM, (2, CCELLS, CCH)),
    ]
    earlier = () if tick == 0 else tuple(kept[:3]) if tick == 2 else tuple(kept)
    start = len(common) + len(added)
    return call(
        functools.partial(keep, tick),
        stashes,
        [SM, VM, VM, ANY, ANY] + [VM if tick == 3 else ANY] * len(added) + [ANY] * len(earlier),
        (
            pltpu.VMEM((CELLS, FCH), BF16),
            pltpu.VMEM((CCELLS, CCH), BF16),
            pltpu.VMEM((FCH, FCH), BF16),
            pltpu.VMEM((CCH, CCH), BF16),
            pltpu.VMEM((4, CELLS, FCH), BF16),
            pltpu.SemaphoreType.DMA((6,)),
        ),
        40_000_000,
        1_000_000,
        {start + i: i for i in range(len(earlier))},
    )(*common, *added, *earlier)


def tied(*values):
    return lax.optimization_barrier(values)


def on_device(
    fine_inflow,
    coarse_inflow,
    fine_entries,
    fine_pending,
    coarse_pending,
    fine_kernels,
    fine_mixing,
    fine_gains,
    fine_shifts,
    coarse_kernel,
    coarse_mixing,
    coarse_gains,
    coarse_shifts,
    descent_kernel,
    upsample_kernel,
):
    place = jnp.stack([lax.axis_index("segment"), lax.axis_index("dp") % 2]).astype(jnp.int32)
    inflow = fine_inflow.reshape(CELLS, FCH)
    cinflow = coarse_inflow.reshape(CCELLS, CCH)
    entries = fine_entries.reshape(TICKS - 1, CELLS, FCH)
    pending = fine_pending.reshape(6, CELLS, FCH)
    cpending = coarse_pending.reshape(2, CCELLS, CCH)
    kernels = fine_kernels.reshape(2, 3, 3 * FCH, FCH)
    ckernel = coarse_kernel.reshape(3, 3 * CCH, CCH)
    mixing = fine_mixing.reshape(FCH, FCH)
    cmixing = coarse_mixing.reshape(CCH, CCH)
    gains, shifts = fine_gains.reshape(2, FCH), fine_shifts.reshape(2, FCH)
    cgains, cshifts = coarse_gains.reshape(1, CCH), coarse_shifts.reshape(1, CCH)
    descent = descent_kernel.reshape(4 * FCH, CCH)
    upsampling = upsample_kernel.transpose(1, 2, 0, 3).reshape(4, CCH, FCH)

    fine_route = [(0, 1), (1, 2), (2, 3), (4, 5), (5, 6), (6, 7)]
    up_route = [(HALF - 1, HALF)]
    coarse_route = [(p, (p + 1) % (2 * HALF)) for p in range(2 * HALF)]
    pairs = [[p, p + HALF] for p in range(HALF)]
    cores = [(i, i ^ 1) for i in range(N_DP)]

    ftile, ctile = (CELLS, FCH), (CCELLS, CCH)
    fine_bf, coarse_bf = pltpu.VMEM(ftile, BF16), pltpu.VMEM(ctile, BF16)
    padded = pltpu.VMEM((CELLS + 2 * SIDE, 3 * FCH), BF16)
    held = pltpu.VMEM((3, 3 * FCH, FCH), BF16)
    conv_flops = 2 * CELLS * 9 * FCH * FCH
    vmem, hbm = pltpu.VMEM, pltpu.HBM

    arrived = raised = carrived = kept = None
    for tick in range(TICKS):
        sending = tick < TICKS - 1
        if tick == 0:
            sources, specs = (inflow, pending, mixing, kernels, cpending), [SM, ANY, ANY, ANY, ANY, ANY]
            more = (pltpu.VMEM((4, CELLS, FCH), BF16), pltpu.SemaphoreType.DMA((5,)))
        else:
            sources = (arrived, raised, entries, upsampling, pending, mixing, kernels)
            specs = [SM, VM, VM, ANY, ANY, ANY, ANY, ANY]
            more = (
                pltpu.VMEM((2, CELLS, 128), F32),
                pltpu.VMEM((4, CCH, FCH), BF16),
                pltpu.SemaphoreType.DMA((4,)),
            )
        h1, pay, *packed = call(
            functools.partial(fine_first, tick),
            [(vmem, ftile, F32), (vmem, (N_DP, 4, 128), F32)] + [(hbm, (4, CELLS, FCH))] * (tick == 0),
            specs,
            (fine_bf, padded, fine_bf, pltpu.VMEM((FCH, FCH), BF16), held, pltpu.SemaphoreType.DMA((6,)), *more),
            conv_flops,
            1_000_000,
        )(place, *sources)

        if tick == 0:
            carrived = cinflow
            pay, later = tied(pay, place)
            skips = lax.all_gather(packed[0], "segment", axis_index_groups=pairs)
        else:
            pay, carrived = tied(pay, carrived)
            later = place
        gathered = lax.all_to_all(pay, "dp", 0, 0, tiled=True)
        hc, mine, other = call(
            functools.partial(coarse_first, tick),
            [(vmem, ctile, F32), (vmem, (4, 128), F32), (vmem, (4, 128), F32)],
            [SM, VM if tick else ANY, ANY, ANY, ANY],
            (
                coarse_bf,
                pltpu.VMEM((3, CCELLS, 3 * CCH), BF16),
                pltpu.VMEM((CCH, CCH), BF16),
                pltpu.VMEM((3, 3 * CCH, CCH), BF16),
                pltpu.SemaphoreType.DMA((7,)),
                coarse_bf,
            ),
            2 * CCELLS * 9 * CCH * CCH,
            1_500_000,
        )(later, carrived, cpending if tick < 2 else skips, cmixing, ckernel)
        theirs = lax.ppermute(other, "dp", cores)
        h2, pay2 = call(
            fine_second,
            [(vmem, ftile, F32), (vmem, (N_DP, 8, 128), F32)],
            [VM, VM, VM, VM, ANY, VM, VM],
            (padded, held, pltpu.SemaphoreType.DMA((3,))),
            conv_flops,
            1_000_000,
        )(gathered, h1, gains, shifts, kernels, mine, theirs)
        if tick > 0:
            pay2, own, cown = tied(pay2, own, cown)
        gathered2 = lax.all_to_all(pay2, "dp", 0, 0, tiled=True)
        if tick == 0:
            gathered2, upsampling = tied(gathered2, upsampling)
        else:
            added = ((pending,), (), (skips,))[tick - 1]
            kept = kept_after(tick - 1, (place, own, cown, mixing, cmixing), added, kept)
            gathered2, *kept = tied(gathered2, *kept)
            if tick == 2:
                fresh = lax.ppermute(kept[3], "segment", [(p + HALF, p) for p in range(HALF)])
        own, cown, *going = call(
            functools.partial(finish, tick),
            [(vmem, ftile), (vmem, ctile)] + ([(vmem, ctile)] if sending else []),
            [SM] + [VM] * 7 + [ANY] * sending,
            (
                pltpu.VMEM((CELLS, 128), F32),
                pltpu.VMEM((CCELLS, 4 * FCH), BF16),
                pltpu.VMEM((4 * FCH, CCH), BF16),
                pltpu.SemaphoreType.DMA,
            ) if sending else (),
            100_000_000,
            1_000_000,
        )(place, gathered2, h2, hc, gains, shifts, cgains, cshifts, *((descent,) if sending else ()))
        if sending:
            raised = lax.ppermute(cown, "segment", up_route)
            arrived = lax.ppermute(own, "segment", fine_route)
            carrived = lax.ppermute(going[0], "segment", coarse_route)
    fstash, cstash, fback, cback = kept_after(
        TICKS - 1, (place, own, cown, mixing, cmixing), (fresh,), kept
    )
    return (
        fstash.reshape(1, TICKS, 1, SIDE, SIDE, FCH),
        cstash.reshape(1, TICKS, 1, CSIDE, CSIDE, CCH),
        fback.reshape(1, 6, 1, SIDE, SIDE, FCH),
        cback.reshape(1, 2, 1, CSIDE, CSIDE, CCH),
    )


def solution(mesh):
    placed = (
        P("segment", "dp", None, None, None),
        P("segment", "dp", None, None, None),
        P(None, "dp", None, None, None),
        P("segment", None, "dp", None, None, None),
        P("segment", None, "dp", None, None, None),
        P("segment", None, None, None, None, None),
        P("segment", None, None),
        P("segment", None, None),
        P("segment", None, None),
        P("segment", None, None, None, None),
        P("segment", None, None),
        P("segment", None),
        P("segment", None),
        P(),
        P(),
    )
    return jax.shard_map(
        on_device,
        mesh=mesh,
        in_specs=placed,
        out_specs=(P("segment", None, "dp", None, None, None),) * 4,
        check_vma=False,
    )
```

```python
import functools

import jax
import jax.numpy as jnp
from jax import lax
from jax.experimental import pallas as pl
from jax.experimental.pallas import tpu as pltpu
from jax.sharding import PartitionSpec as P

EPSILON = 1e-05
BF16 = jnp.bfloat16
F32 = jnp.float32
LIMIT = 24 * 1024 * 1024

SIDE, CSIDE = 16, 8
CELLS, CCELLS = SIDE * SIDE, CSIDE * CSIDE
FCH, CCH = 256, 512
N_DP = 32
HALF = 4
LAST = 2 * HALF - 1
TICKS = 4


def call(body, outs, in_specs, scratch=(), flops=0, moved=0, aliases=None):
    kernel = pl.pallas_call(
        body,
        out_shape=[space(*rest) if len(rest) == 2 else space(*rest, BF16) for space, *rest in outs],
        in_specs=in_specs,
        out_specs=[VM if space is pltpu.VMEM else ANY for space, *_ in outs],
        scratch_shapes=list(scratch),
        input_output_aliases=aliases or {},
        compiler_params=pltpu.CompilerParams(vmem_limit_bytes=LIMIT),
        cost_estimate=pl.CostEstimate(flops=flops, bytes_accessed=moved, transcendentals=0),
    )
    spaces = {id(VM): pltpu.VMEM, id(ANY): pltpu.HBM}

    def placed(spec, x):
        return pltpu.with_memory_space_constraint(x, spaces[id(spec)]) if id(spec) in spaces else x

    return lambda *args: kernel(*[placed(spec, arg) for spec, arg in zip(in_specs, args, strict=True)])


VM = pl.BlockSpec(memory_space=pltpu.VMEM)
SM = pl.BlockSpec(memory_space=pltpu.SMEM)
ANY = pl.BlockSpec(memory_space=pl.ANY)


def dot(a, b):
    return jnp.dot(a, b, preferred_element_type=F32)


def lanes(rows):
    return jnp.concatenate([rows[i : i + 1] for i in range(rows.shape[0])], axis=1)


def rows_of(line):
    return [line[:, i : i + 128] for i in range(0, line.shape[1], 128)]


def with_neighbours(x, width):
    count = x.shape[0]
    column = lax.broadcasted_iota(jnp.int32, x.shape, 0) & (width - 1)
    left = jnp.where(column == 0, 0.0, pltpu.roll(x, 1, 0))
    right = jnp.where(column == width - 1, 0.0, pltpu.roll(x, count - 1, 0))
    return left, x, right


class Streamed:
    def __init__(self, source, held, sems):
        self.held = held
        self.copies = [
            pltpu.make_async_copy(source.at[i], held.at[i], sems.at[i]) for i in range(held.shape[0])
        ]

    def start(self):
        for copy in self.copies:
            copy.start()
        return self

    def __getitem__(self, i):
        self.copies[i].wait()
        return self.held[i]


def fine_convolution(x, padded, kernel):
    edge = jnp.zeros((SIDE, 3 * FCH), BF16)
    padded[0:SIDE, :] = edge
    padded[SIDE + CELLS : 2 * SIDE + CELLS, :] = edge
    for i, piece in enumerate(with_neighbours(x, SIDE)):
        padded[SIDE : SIDE + CELLS, i * FCH : (i + 1) * FCH] = piece.astype(BF16)
    total = dot(padded[0:CELLS, :], kernel[0])
    total += dot(padded[SIDE : SIDE + CELLS, :], kernel[1])
    total += dot(padded[2 * SIDE : 2 * SIDE + CELLS, :], kernel[2])
    return total


def local_moments(h):
    mean = jnp.sum(h, axis=0, keepdims=True) * (1.0 / h.shape[0])
    away = h - mean
    return mean, jnp.sum(away * away, axis=0, keepdims=True)


def merged(pieces, cells_each):
    count = len(pieces)
    k = pieces[0].shape[0] // 2
    total = functools.reduce(jnp.add, pieces)
    mean = total * (1.0 / count)
    drift = functools.reduce(jnp.add, [jnp.square(piece - mean) for piece in pieces])
    spread = (total[k:] + cells_each * drift[:k]) * (1.0 / (count * cells_each))
    return lanes(mean[:k]), lanes(spread)


def activated(h, mean, spread, gain, shift):
    return jnp.maximum((h - mean) * lax.rsqrt(spread + EPSILON) * gain + shift, 0.0)


def fine_first(tick, *refs):
    if tick == 0:
        place, inflow, pending, mixing, kernels = refs[:5]
        refs = refs[5:]
    else:
        place, arrived, raised_in, entries, raising, pending, mixing, kernels = refs[:8]
        refs = refs[8:]
    h_ref, pay_ref = refs[:2]
    if tick == 0:
        packed, held, second = refs[2:5]
        x_ref, padded, skip_ref, mix_ref, sems, staged, pack_sems = refs[5:]
    else:
        x_ref, padded, skip_ref, mix_ref, sems, spread_ref, up_ref, up_sems = refs[2:]
    segment = place[0]
    kernel = Streamed(kernels.at[0], held, sems.at[pl.ds(0, 3)]) if tick == 0 else kernels
    skip = pltpu.make_async_copy(pending.at[tick], skip_ref, sems.at[3])
    mix = pltpu.make_async_copy(mixing, mix_ref, sems.at[4])

    if tick == 0:
        x = pltpu.make_async_copy(inflow, x_ref, sems.at[5])
        x.start()
    else:
        up = Streamed(raising, up_ref, up_sems)

        @pl.when(segment == HALF)
        def _():
            up.start()

        @pl.when(segment == 0)
        def _():
            pltpu.make_async_copy(entries.at[tick - 1], x_ref, sems.at[5]).start()

    @pl.when(segment >= HALF)
    def _():
        mix.start()
        skip.start()

    if tick == 0:
        kernel.start()
        onward = pltpu.make_async_copy(kernels.at[1], second, pack_sems.at[5])
        onward.start()
        loads = [pltpu.make_async_copy(pending.at[slot], staged.at[slot], pack_sems.at[slot]) for slot in range(4)]
        store = pltpu.make_async_copy(staged, packed, pack_sems.at[4])

        @pl.when(segment < HALF)
        def _():
            for copy in loads:
                copy.start()

    if tick == 0:
        x.wait()
    else:

        @pl.when(segment == 0)
        def _():
            pltpu.make_async_copy(entries.at[tick - 1], x_ref, sems.at[5]).wait()

        @pl.when((segment != 0) & (segment != HALF))
        def _():
            x_ref[...] = arrived[...]

        @pl.when(segment == HALF)
        def _():
            for part in range(4):
                raised = dot(raised_in[...], up[part])
                for i in range(CSIDE):
                    start = (2 * i + part // 2) * SIDE + part % 2
                    for p in range(FCH // 128):
                        spread_ref[p, pl.ds(start, CSIDE, stride=2), :] = raised[
                            i * CSIDE : (i + 1) * CSIDE, p * 128 : (p + 1) * 128
                        ]
            for p in range(FCH // 128):
                x_ref[:, p * 128 : (p + 1) * 128] = spread_ref[p].astype(BF16)

    @pl.when(segment >= HALF)
    def _():
        skip.wait()
        mix.wait()
        x_ref[...] = (dot(x_ref[...], mix_ref[...]) + skip_ref[...].astype(F32)).astype(BF16)

    if tick == 0:

        @pl.when(segment < HALF)
        def _():
            for copy in loads:
                copy.wait()
            store.start()

    h = fine_convolution(x_ref[...].astype(F32), padded, kernel)
    h_ref[...] = h
    mean, spread = local_moments(h)
    pay = jnp.concatenate(rows_of(mean) + rows_of(spread), axis=0)
    pay_ref[...] = jnp.broadcast_to(pay[None], pay_ref.shape)
    if tick == 0:
        onward.wait()

        @pl.when(segment < HALF)
        def _():
            store.wait()


def coarse_first(tick, *refs):
    place, arrived, pending, mixing, kernels = refs[:5]
    h_ref, mine_ref, other_ref, x_ref, padded, mix_ref, held, sems, skip_ref = refs[5:]
    kernel = Streamed(kernels, held, sems.at[pl.ds(3, 3)])
    skips = [pltpu.make_async_copy(pending.at[tick % 2], skip_ref, sems.at[1])]
    segment = place[0]
    mix = pltpu.make_async_copy(mixing, mix_ref, sems.at[0])

    @pl.when(segment < HALF)
    def _():
        mix.start()
        for skip in skips:
            skip.start()

    if tick == 0:
        fetch = pltpu.make_async_copy(arrived, x_ref, sems.at[2])
        fetch.start()
    kernel.start()
    if tick == 0:
        fetch.wait()
    else:
        x_ref[...] = arrived[...]
    @pl.when(segment < HALF)
    def _():
        mix.wait()
        for skip in skips:
            skip.wait()
        x_ref[...] = (dot(x_ref[...], mix_ref[...]) + skip_ref[...].astype(F32)).astype(BF16)

    edge = jnp.zeros((CSIDE, CCH), F32)
    for i, piece in enumerate(with_neighbours(x_ref[...].astype(F32), CSIDE)):
        columns = slice(i * CCH, (i + 1) * CCH)
        padded[0, :, columns] = jnp.concatenate([edge, piece[: CCELLS - CSIDE]], axis=0).astype(BF16)
        padded[1, :, columns] = piece.astype(BF16)
        padded[2, :, columns] = jnp.concatenate([piece[CSIDE:], edge], axis=0).astype(BF16)
    h = dot(padded[0], kernel[0])
    h += dot(padded[1], kernel[1])
    h += dot(padded[2], kernel[2])
    h_ref[...] = h
    mean, spread = local_moments(h)
    mean, spread = rows_of(mean), rows_of(spread)
    first = jnp.concatenate(mean[:2] + spread[:2], axis=0)
    second = jnp.concatenate(mean[2:] + spread[2:], axis=0)
    is_first = place[1] == 0
    mine_ref[...] = jnp.where(is_first, first, second)
    other_ref[...] = jnp.where(is_first, second, first)


def fine_second(gathered, h_ref, gains, shifts, kernel, mine, theirs, out_ref, pay_ref, padded):
    mean, spread = merged([gathered[i] for i in range(N_DP)], float(CELLS))
    x = activated(h_ref[...], mean, spread, gains[0:1], shifts[0:1]).astype(BF16)
    h = fine_convolution(x.astype(F32), padded, kernel)
    out_ref[...] = h
    mean, spread = local_moments(h)
    a, b = mine[...], theirs[...]
    pair_mean = (a[:2] + b[:2]) * 0.5
    pair_spread = a[2:] + b[2:] + jnp.square(a[:2] - b[:2]) * (0.5 * CCELLS)
    pay = jnp.concatenate(rows_of(mean) + rows_of(spread) + [pair_mean, pair_spread], axis=0)
    pay_ref[...] = jnp.broadcast_to(pay[None], pay_ref.shape)


def finish(tick, gathered, h_ref, hc_ref, gains, shifts, cgains, cshifts, fine_ref, coarse_ref):
    mean, spread = merged([gathered[i, 0:4] for i in range(N_DP)], float(CELLS))
    fine_ref[...] = activated(h_ref[...], mean, spread, gains[1:2], shifts[1:2]).astype(BF16)
    mean0, spread0 = merged([gathered[i, 4:8] for i in range(0, N_DP, 2)], 2.0 * CCELLS)
    mean1, spread1 = merged([gathered[i, 4:8] for i in range(1, N_DP, 2)], 2.0 * CCELLS)
    mean = jnp.concatenate([mean0, mean1], axis=1)
    spread = jnp.concatenate([spread0, spread1], axis=1)
    coarse_ref[...] = activated(hc_ref[...], mean, spread, cgains[...], cshifts[...]).astype(BF16)


def coarse_sent(place, fine, coarse, descent, going, fine32, packed, down_ref, sem):
    segment = place[0]

    @pl.when(segment != HALF - 1)
    def _():
        going[...] = coarse[...]

    @pl.when(segment == HALF - 1)
    def _():
        fetch = pltpu.make_async_copy(descent, down_ref, sem)
        fetch.start()
        for p in range(FCH // 128):
            fine32[...] = fine[:, p * 128 : (p + 1) * 128].astype(F32)
            for a in range(2):
                for c in range(2):
                    taken = [fine32[pl.ds((2 * i + a) * SIDE + c, CSIDE, stride=2), :] for i in range(CSIDE)]
                    column = (2 * a + c) * FCH + p * 128
                    packed[:, column : column + 128] = jnp.concatenate(taken, axis=0).astype(BF16)
        fetch.wait()
        going[...] = dot(packed[...], down_ref[...]).astype(BF16)


def keep(tick, *refs):
    place, fine, coarse, mixing, cmixing = refs[:5]
    refs = refs[5:]
    if tick != 1:
        extra, refs = refs[0], refs[1:]
    fstash, cstash, fback, ctarget, term, cterm, mix_ref, cmix_ref, staged, sems = refs[(0, 4, 3, 4)[tick] :]
    segment = place[0]
    copies = [
        pltpu.make_async_copy(fine, fstash.at[tick], sems.at[0]),
        pltpu.make_async_copy(coarse, cstash.at[tick], sems.at[1]),
    ]
    for copy in copies:
        copy.start()
    if tick == 0:
        load = pltpu.make_async_copy(extra.at[4:6], staged.at[0:2], sems.at[2])
        load.start()

    @pl.when(segment < HALF)
    def _():
        fetch = pltpu.make_async_copy(mixing, mix_ref, sems.at[3])
        fetch.start()
        if tick == 3:
            ccopy = pltpu.make_async_copy(extra, ctarget, sems.at[5])
            ccopy.start()
        fetch.wait()
        term[...] = dot(fine[...], mix_ref[...]).astype(BF16)
        copy = pltpu.make_async_copy(term, fback.at[2 + tick], sems.at[4])
        copy.start()
        if tick == 3:
            ccopy.wait()
        copy.wait()

    @pl.when(segment >= HALF)
    def _():
        fetch = pltpu.make_async_copy(cmixing, cmix_ref, sems.at[3])
        fetch.start()
        if tick == 2:
            received = pltpu.make_async_copy(extra, staged, sems.at[4])
            received.start()
        fetch.wait()
        cterm[...] = dot(coarse[...], cmix_ref[...]).astype(BF16)
        copy = pltpu.make_async_copy(cterm, ctarget.at[tick % 2], sems.at[5])
        copy.start()
        if tick == 2:
            received.wait()
            stored = pltpu.make_async_copy(staged, fback.at[2:6], sems.at[4])
            stored.start()
            stored.wait()
        copy.wait()

    if tick == 0:
        load.wait()
        store = pltpu.make_async_copy(staged.at[0:2], fback.at[0:2], sems.at[2])
        store.start()
        store.wait()
    for copy in copies:
        copy.wait()


def kept_after(tick, common, added, kept):
    stashes = [
        (pltpu.HBM, (TICKS, CELLS, FCH)),
        (pltpu.HBM, (TICKS, CCELLS, CCH)),
        (pltpu.HBM, (6, CELLS, FCH)),
        (pltpu.HBM, (2, CCELLS, CCH)),
    ]
    earlier = () if tick == 0 else tuple(kept[:3]) if tick == 2 else tuple(kept)
    start = len(common) + len(added)
    return call(
        functools.partial(keep, tick),
        stashes,
        [SM, VM, VM, ANY, ANY] + [VM if tick == 3 else ANY] * len(added) + [ANY] * len(earlier),
        (
            pltpu.VMEM((CELLS, FCH), BF16),
            pltpu.VMEM((CCELLS, CCH), BF16),
            pltpu.VMEM((FCH, FCH), BF16),
            pltpu.VMEM((CCH, CCH), BF16),
            pltpu.VMEM((4, CELLS, FCH), BF16),
            pltpu.SemaphoreType.DMA((6,)),
        ),
        40_000_000,
        1_000_000,
        {start + i: i for i in range(len(earlier))},
    )(*common, *added, *earlier)


def tied(*values):
    return lax.optimization_barrier(values)


def on_device(
    fine_inflow,
    coarse_inflow,
    fine_entries,
    fine_pending,
    coarse_pending,
    fine_kernels,
    fine_mixing,
    fine_gains,
    fine_shifts,
    coarse_kernel,
    coarse_mixing,
    coarse_gains,
    coarse_shifts,
    descent_kernel,
    upsample_kernel,
):
    place = jnp.stack([lax.axis_index("segment"), lax.axis_index("dp") % 2]).astype(jnp.int32)
    inflow = fine_inflow.reshape(CELLS, FCH)
    cinflow = coarse_inflow.reshape(CCELLS, CCH)
    entries = fine_entries.reshape(TICKS - 1, CELLS, FCH)
    pending = fine_pending.reshape(6, CELLS, FCH)
    cpending = coarse_pending.reshape(2, CCELLS, CCH)
    kernels = fine_kernels.reshape(2, 3, 3 * FCH, FCH)
    ckernel = coarse_kernel.reshape(3, 3 * CCH, CCH)
    mixing = fine_mixing.reshape(FCH, FCH)
    cmixing = coarse_mixing.reshape(CCH, CCH)
    gains, shifts = fine_gains.reshape(2, FCH), fine_shifts.reshape(2, FCH)
    cgains, cshifts = coarse_gains.reshape(1, CCH), coarse_shifts.reshape(1, CCH)
    descent = descent_kernel.reshape(4 * FCH, CCH)
    upsampling = upsample_kernel.transpose(1, 2, 0, 3).reshape(4, CCH, FCH)

    fine_route = [(0, 1), (1, 2), (2, 3), (4, 5), (5, 6), (6, 7)]
    up_route = [(HALF - 1, HALF)]
    coarse_route = [(p, (p + 1) % (2 * HALF)) for p in range(2 * HALF)]
    to_decoder = [(p, p + HALF) for p in range(HALF)]
    to_encoder = [(p + HALF, p) for p in range(HALF)]
    cores = [(i, i ^ 1) for i in range(N_DP)]

    ftile, ctile = (CELLS, FCH), (CCELLS, CCH)
    fine_bf, coarse_bf = pltpu.VMEM(ftile, BF16), pltpu.VMEM(ctile, BF16)
    padded = pltpu.VMEM((CELLS + 2 * SIDE, 3 * FCH), BF16)
    vmem, hbm = pltpu.VMEM, pltpu.HBM
    kernel_kept = (vmem, (3, 3 * FCH, FCH))
    conv_flops = 2 * CELLS * 9 * FCH * FCH

    arrived = raised = carrived = kept = None
    for tick in range(TICKS):
        sending = tick < TICKS - 1
        if tick == 0:
            sources, specs = (inflow, pending, mixing, kernels), [SM, ANY, ANY, ANY, ANY]
            more = (pltpu.VMEM((4, CELLS, FCH), BF16), pltpu.SemaphoreType.DMA((6,)))
        else:
            sources = (arrived, raised, entries, upsampling, pending, mixing, kernel_one)
            specs = [SM, VM, VM, ANY, ANY, ANY, ANY, VM]
            more = (
                pltpu.VMEM((2, CELLS, 128), F32),
                pltpu.VMEM((4, CCH, FCH), BF16),
                pltpu.SemaphoreType.DMA((4,)),
            )
        h1, pay, *handed = call(
            functools.partial(fine_first, tick),
            [(vmem, ftile, F32), (vmem, (N_DP, 4, 128), F32)] + ([(hbm, (4, CELLS, FCH)), kernel_kept, kernel_kept] if tick == 0 else []),
            specs,
            (fine_bf, padded, fine_bf, pltpu.VMEM((FCH, FCH), BF16), pltpu.SemaphoreType.DMA((6,)), *more),
            conv_flops,
            1_000_000,
        )(place, *sources)

        if tick == 0:
            carrived = cinflow
            packed, kernel_one, kernel_two = handed
            pay, later = tied(pay, place)
            skips = lax.ppermute(packed, "segment", to_decoder)
        else:
            pay, carrived = tied(pay, carrived)
            later = place
        gathered = lax.all_to_all(pay, "dp", 0, 0, tiled=True)
        hc, mine, other = call(
            functools.partial(coarse_first, tick),
            [(vmem, ctile, F32), (vmem, (4, 128), F32), (vmem, (4, 128), F32)],
            [SM, VM if tick else ANY, ANY, ANY, ANY],
            (
                coarse_bf,
                pltpu.VMEM((3, CCELLS, 3 * CCH), BF16),
                pltpu.VMEM((CCH, CCH), BF16),
                pltpu.VMEM((3, 3 * CCH, CCH), BF16),
                pltpu.SemaphoreType.DMA((7,)),
                coarse_bf,
            ),
            2 * CCELLS * 9 * CCH * CCH,
            1_500_000,
        )(later, carrived, cpending if tick < 2 else cskips, cmixing, ckernel)
        theirs = lax.ppermute(other, "dp", cores)
        if tick == 2:
            gathered, skips = tied(gathered, skips)
        h2, pay2 = call(
            fine_second,
            [(vmem, ftile, F32), (vmem, (N_DP, 8, 128), F32)],
            [VM] * 7,
            (padded,),
            conv_flops,
            1_000_000,
        )(gathered, h1, gains, shifts, kernel_two, mine, theirs)
        if tick > 0:
            pay2, own, cown = tied(pay2, own, cown)
        gathered2 = lax.all_to_all(pay2, "dp", 0, 0, tiled=True)
        if tick == 0:
            cskips = lax.ppermute(tied(cpending, pay2)[0], "segment", to_encoder)
            gathered2, upsampling, cskips = tied(gathered2, upsampling, cskips)
        else:
            added = ((pending,), (), (skips,))[tick - 1]
            kept = kept_after(tick - 1, (place, own, cown, mixing, cmixing), added, kept)
            gathered2, *kept = tied(gathered2, *kept)
            if tick == 2:
                fresh = lax.ppermute(kept[3], "segment", to_encoder)
        own, cown = call(
            functools.partial(finish, tick),
            [(vmem, ftile), (vmem, ctile)],
            [VM] * 7,
            (),
            1_000_000,
            1_000_000,
        )(gathered2, h2, hc, gains, shifts, cgains, cshifts)
        if sending:
            raised = lax.ppermute(cown, "segment", up_route)
            arrived = lax.ppermute(own, "segment", fine_route)
            (going,) = call(
                coarse_sent,
                [(vmem, ctile)],
                [SM, VM, VM, ANY],
                (
                    pltpu.VMEM((CELLS, 128), F32),
                    pltpu.VMEM((CCELLS, 4 * FCH), BF16),
                    pltpu.VMEM((4 * FCH, CCH), BF16),
                    pltpu.SemaphoreType.DMA,
                ),
                100_000_000,
                1_000_000,
            )(place, own, cown, descent)
            carrived = lax.ppermute(going, "segment", coarse_route)
    fstash, cstash, fback, cback = kept_after(
        TICKS - 1, (place, own, cown, mixing, cmixing), (fresh,), kept
    )
    return (
        fstash.reshape(1, TICKS, 1, SIDE, SIDE, FCH),
        cstash.reshape(1, TICKS, 1, CSIDE, CSIDE, CCH),
        fback.reshape(1, 6, 1, SIDE, SIDE, FCH),
        cback.reshape(1, 2, 1, CSIDE, CSIDE, CCH),
    )


def solution(mesh):
    placed = (
        P("segment", "dp", None, None, None),
        P("segment", "dp", None, None, None),
        P(None, "dp", None, None, None),
        P("segment", None, "dp", None, None, None),
        P("segment", None, "dp", None, None, None),
        P("segment", None, None, None, None, None),
        P("segment", None, None),
        P("segment", None, None),
        P("segment", None, None),
        P("segment", None, None, None, None),
        P("segment", None, None),
        P("segment", None),
        P("segment", None),
        P(),
        P(),
    )
    return jax.shard_map(
        on_device,
        mesh=mesh,
        in_specs=placed,
        out_specs=(P("segment", None, "dp", None, None, None),) * 4,
        check_vma=False,
    )
```

```python
import functools

import jax
import jax.numpy as jnp
from jax import lax
from jax.experimental import pallas as pl
from jax.experimental.pallas import tpu as pltpu
from jax.sharding import PartitionSpec as P

EPSILON = 1e-05
BF16 = jnp.bfloat16
F32 = jnp.float32
LIMIT = 24 * 1024 * 1024

SIDE, CSIDE = 16, 8
CELLS, CCELLS = SIDE * SIDE, CSIDE * CSIDE
FCH, CCH = 256, 512
N_DP = 32
HALF = 4
LAST = 2 * HALF - 1
TICKS = 4


def call(body, outs, in_specs, scratch=(), flops=0, moved=0, aliases=None):
    kernel = pl.pallas_call(
        body,
        out_shape=[space(*rest) if len(rest) == 2 else space(*rest, BF16) for space, *rest in outs],
        in_specs=in_specs,
        out_specs=[VM if space is pltpu.VMEM else ANY for space, *_ in outs],
        scratch_shapes=list(scratch),
        input_output_aliases=aliases or {},
        compiler_params=pltpu.CompilerParams(vmem_limit_bytes=LIMIT),
        cost_estimate=pl.CostEstimate(flops=flops, bytes_accessed=moved, transcendentals=0),
    )
    spaces = {id(VM): pltpu.VMEM, id(ANY): pltpu.HBM}

    def placed(spec, x):
        return pltpu.with_memory_space_constraint(x, spaces[id(spec)]) if id(spec) in spaces else x

    return lambda *args: kernel(*[placed(spec, arg) for spec, arg in zip(in_specs, args, strict=True)])


VM = pl.BlockSpec(memory_space=pltpu.VMEM)
SM = pl.BlockSpec(memory_space=pltpu.SMEM)
ANY = pl.BlockSpec(memory_space=pl.ANY)


def dot(a, b):
    return jnp.dot(a, b, preferred_element_type=F32)


def lanes(rows):
    return jnp.concatenate([rows[i : i + 1] for i in range(rows.shape[0])], axis=1)


def rows_of(line):
    return [line[:, i : i + 128] for i in range(0, line.shape[1], 128)]


def with_neighbours(x, width):
    count = x.shape[0]
    column = lax.broadcasted_iota(jnp.int32, x.shape, 0) & (width - 1)
    left = jnp.where(column == 0, 0.0, pltpu.roll(x, 1, 0))
    right = jnp.where(column == width - 1, 0.0, pltpu.roll(x, count - 1, 0))
    return left, x, right


class Streamed:
    def __init__(self, source, held, sems):
        self.held = held
        self.copies = [
            pltpu.make_async_copy(source.at[i], held.at[i], sems.at[i]) for i in range(held.shape[0])
        ]

    def start(self):
        for copy in self.copies:
            copy.start()
        return self

    def __getitem__(self, i):
        self.copies[i].wait()
        return self.held[i]


def fine_convolution(x, padded, kernel):
    edge = jnp.zeros((SIDE, 3 * FCH), BF16)
    padded[0:SIDE, :] = edge
    padded[SIDE + CELLS : 2 * SIDE + CELLS, :] = edge
    for i, piece in enumerate(with_neighbours(x, SIDE)):
        padded[SIDE : SIDE + CELLS, i * FCH : (i + 1) * FCH] = piece.astype(BF16)
    total = dot(padded[0:CELLS, :], kernel[0])
    total += dot(padded[SIDE : SIDE + CELLS, :], kernel[1])
    total += dot(padded[2 * SIDE : 2 * SIDE + CELLS, :], kernel[2])
    return total


def local_moments(h):
    mean = jnp.sum(h, axis=0, keepdims=True) * (1.0 / h.shape[0])
    away = h - mean
    return mean, jnp.sum(away * away, axis=0, keepdims=True)


def merged(pieces, cells_each):
    count = len(pieces)
    k = pieces[0].shape[0] // 2
    total = functools.reduce(jnp.add, pieces)
    mean = total * (1.0 / count)
    drift = functools.reduce(jnp.add, [jnp.square(piece - mean) for piece in pieces])
    spread = (total[k:] + cells_each * drift[:k]) * (1.0 / (count * cells_each))
    return lanes(mean[:k]), lanes(spread)


def activated(h, mean, spread, gain, shift):
    return jnp.maximum((h - mean) * lax.rsqrt(spread + EPSILON) * gain + shift, 0.0)


def fine_first(tick, *refs):
    if tick == 0:
        place, inflow, pending, mixing, kernels = refs[:5]
        refs = refs[5:]
    else:
        place, arrived, raised_in, entries, raising, pending, mixing, kernels = refs[:8]
        refs = refs[8:]
    h_ref, pay_ref = refs[:2]
    if tick == 0:
        packed, held, second = refs[2:5]
        x_ref, padded, skip_ref, mix_ref, sems, staged, pack_sems = refs[5:]
    else:
        x_ref, padded, skip_ref, mix_ref, sems, spread_ref, up_ref, up_sems = refs[2:]
    segment = place[0]
    kernel = Streamed(kernels.at[0], held, sems.at[pl.ds(0, 3)]) if tick == 0 else kernels
    skip = pltpu.make_async_copy(pending.at[tick], skip_ref, sems.at[3])
    mix = pltpu.make_async_copy(mixing, mix_ref, sems.at[4])

    if tick == 0:
        x = pltpu.make_async_copy(inflow, x_ref, sems.at[5])
        x.start()
    else:
        up = Streamed(raising, up_ref, up_sems)

        @pl.when(segment == HALF)
        def _():
            up.start()

        @pl.when(segment == 0)
        def _():
            pltpu.make_async_copy(entries.at[tick - 1], x_ref, sems.at[5]).start()

    @pl.when(segment >= HALF)
    def _():
        mix.start()
        skip.start()

    if tick == 0:
        kernel.start()
        onward = pltpu.make_async_copy(kernels.at[1], second, pack_sems.at[5])
        onward.start()
        loads = [pltpu.make_async_copy(pending.at[slot], staged.at[slot], pack_sems.at[slot]) for slot in range(4)]
        store = pltpu.make_async_copy(staged, packed, pack_sems.at[4])

        @pl.when(segment < HALF)
        def _():
            for copy in loads:
                copy.start()

    if tick == 0:
        x.wait()
    else:

        @pl.when(segment == 0)
        def _():
            pltpu.make_async_copy(entries.at[tick - 1], x_ref, sems.at[5]).wait()

        @pl.when((segment != 0) & (segment != HALF))
        def _():
            x_ref[...] = arrived[...]

        @pl.when(segment == HALF)
        def _():
            for part in range(4):
                raised = dot(raised_in[...], up[part])
                for i in range(CSIDE):
                    start = (2 * i + part // 2) * SIDE + part % 2
                    for p in range(FCH // 128):
                        spread_ref[p, pl.ds(start, CSIDE, stride=2), :] = raised[
                            i * CSIDE : (i + 1) * CSIDE, p * 128 : (p + 1) * 128
                        ]
            for p in range(FCH // 128):
                x_ref[:, p * 128 : (p + 1) * 128] = spread_ref[p].astype(BF16)

    @pl.when(segment >= HALF)
    def _():
        skip.wait()
        mix.wait()
        x_ref[...] = (dot(x_ref[...], mix_ref[...]) + skip_ref[...].astype(F32)).astype(BF16)

    if tick == 0:

        @pl.when(segment < HALF)
        def _():
            for copy in loads:
                copy.wait()
            store.start()

    h = fine_convolution(x_ref[...].astype(F32), padded, kernel)
    h_ref[...] = h
    mean, spread = local_moments(h)
    pay = jnp.concatenate(rows_of(mean) + rows_of(spread), axis=0)
    pay_ref[...] = jnp.broadcast_to(pay[None], pay_ref.shape)
    if tick == 0:
        onward.wait()

        @pl.when(segment < HALF)
        def _():
            store.wait()


def coarse_first(tick, *refs):
    place, arrived, pending, mixing, kernels = refs[:5]
    h_ref, mine_ref, other_ref, x_ref, padded, mix_ref, held, sems, skip_ref = refs[5:]
    kernel = Streamed(kernels, held, sems.at[pl.ds(3, 3)])
    skips = [pltpu.make_async_copy(pending.at[tick % 2], skip_ref, sems.at[1])]
    segment = place[0]
    mix = pltpu.make_async_copy(mixing, mix_ref, sems.at[0])

    @pl.when(segment < HALF)
    def _():
        mix.start()
        for skip in skips:
            skip.start()

    if tick == 0:
        fetch = pltpu.make_async_copy(arrived, x_ref, sems.at[2])
        fetch.start()
    kernel.start()
    if tick == 0:
        fetch.wait()
    else:
        x_ref[...] = arrived[...]
    @pl.when(segment < HALF)
    def _():
        mix.wait()
        for skip in skips:
            skip.wait()
        x_ref[...] = (dot(x_ref[...], mix_ref[...]) + skip_ref[...].astype(F32)).astype(BF16)

    edge = jnp.zeros((CSIDE, CCH), F32)
    for i, piece in enumerate(with_neighbours(x_ref[...].astype(F32), CSIDE)):
        columns = slice(i * CCH, (i + 1) * CCH)
        padded[0, :, columns] = jnp.concatenate([edge, piece[: CCELLS - CSIDE]], axis=0).astype(BF16)
        padded[1, :, columns] = piece.astype(BF16)
        padded[2, :, columns] = jnp.concatenate([piece[CSIDE:], edge], axis=0).astype(BF16)
    h = dot(padded[0], kernel[0])
    h += dot(padded[1], kernel[1])
    h += dot(padded[2], kernel[2])
    h_ref[...] = h
    mean, spread = local_moments(h)
    mean, spread = rows_of(mean), rows_of(spread)
    first = jnp.concatenate(mean[:2] + spread[:2], axis=0)
    second = jnp.concatenate(mean[2:] + spread[2:], axis=0)
    is_first = place[1] == 0
    mine_ref[...] = jnp.where(is_first, first, second)
    other_ref[...] = jnp.where(is_first, second, first)


def fine_second(gathered, h_ref, gains, shifts, kernel, mine, theirs, out_ref, pay_ref, padded):
    mean, spread = merged([gathered[i] for i in range(N_DP)], float(CELLS))
    x = activated(h_ref[...], mean, spread, gains[0:1], shifts[0:1]).astype(BF16)
    h = fine_convolution(x.astype(F32), padded, kernel)
    out_ref[...] = h
    mean, spread = local_moments(h)
    a, b = mine[...], theirs[...]
    pair_mean = (a[:2] + b[:2]) * 0.5
    pair_spread = a[2:] + b[2:] + jnp.square(a[:2] - b[:2]) * (0.5 * CCELLS)
    pay = jnp.concatenate(rows_of(mean) + rows_of(spread) + [pair_mean, pair_spread], axis=0)
    pay_ref[...] = jnp.broadcast_to(pay[None], pay_ref.shape)


def finish(tick, gathered, h_ref, hc_ref, gains, shifts, cgains, cshifts, fine_ref, coarse_ref):
    mean, spread = merged([gathered[i, 0:4] for i in range(N_DP)], float(CELLS))
    fine_ref[...] = activated(h_ref[...], mean, spread, gains[1:2], shifts[1:2]).astype(BF16)
    mean0, spread0 = merged([gathered[i, 4:8] for i in range(0, N_DP, 2)], 2.0 * CCELLS)
    mean1, spread1 = merged([gathered[i, 4:8] for i in range(1, N_DP, 2)], 2.0 * CCELLS)
    mean = jnp.concatenate([mean0, mean1], axis=1)
    spread = jnp.concatenate([spread0, spread1], axis=1)
    coarse_ref[...] = activated(hc_ref[...], mean, spread, cgains[...], cshifts[...]).astype(BF16)


def coarse_sent(place, fine, coarse, descent, going, fine32, packed, down_ref, sem):
    segment = place[0]

    @pl.when(segment != HALF - 1)
    def _():
        going[...] = coarse[...]

    @pl.when(segment == HALF - 1)
    def _():
        fetch = pltpu.make_async_copy(descent, down_ref, sem)
        fetch.start()
        for p in range(FCH // 128):
            fine32[...] = fine[:, p * 128 : (p + 1) * 128].astype(F32)
            for a in range(2):
                for c in range(2):
                    taken = [fine32[pl.ds((2 * i + a) * SIDE + c, CSIDE, stride=2), :] for i in range(CSIDE)]
                    column = (2 * a + c) * FCH + p * 128
                    packed[:, column : column + 128] = jnp.concatenate(taken, axis=0).astype(BF16)
        fetch.wait()
        going[...] = dot(packed[...], down_ref[...]).astype(BF16)


def keep(tick, *refs):
    place, fine, coarse, mixing, cmixing = refs[:5]
    refs = refs[5:]
    if tick != 1:
        extra, refs = refs[0], refs[1:]
    fstash, cstash, fback, ctarget, term, cterm, mix_ref, cmix_ref, staged, sems = refs[(0, 4, 3, 4)[tick] :]
    segment = place[0]
    copies = [
        pltpu.make_async_copy(fine, fstash.at[tick], sems.at[0]),
        pltpu.make_async_copy(coarse, cstash.at[tick], sems.at[1]),
    ]
    for copy in copies:
        copy.start()
    if tick == 0:
        load = pltpu.make_async_copy(extra.at[4:6], staged.at[0:2], sems.at[2])
        load.start()

    @pl.when(segment < HALF)
    def _():
        fetch = pltpu.make_async_copy(mixing, mix_ref, sems.at[3])
        fetch.start()
        if tick == 3:
            ccopy = pltpu.make_async_copy(extra, ctarget, sems.at[5])
            ccopy.start()
        fetch.wait()
        term[...] = dot(fine[...], mix_ref[...]).astype(BF16)
        copy = pltpu.make_async_copy(term, fback.at[2 + tick], sems.at[4])
        copy.start()
        if tick == 3:
            ccopy.wait()
        copy.wait()

    @pl.when(segment >= HALF)
    def _():
        fetch = pltpu.make_async_copy(cmixing, cmix_ref, sems.at[3])
        fetch.start()
        if tick == 2:
            received = pltpu.make_async_copy(extra, staged, sems.at[4])
            received.start()
        fetch.wait()
        cterm[...] = dot(coarse[...], cmix_ref[...]).astype(BF16)
        copy = pltpu.make_async_copy(cterm, ctarget.at[tick % 2], sems.at[5])
        copy.start()
        if tick == 2:
            received.wait()
            stored = pltpu.make_async_copy(staged, fback.at[2:6], sems.at[4])
            stored.start()
            stored.wait()
        copy.wait()

    if tick == 0:
        load.wait()
        store = pltpu.make_async_copy(staged.at[0:2], fback.at[0:2], sems.at[2])
        store.start()
        store.wait()
    for copy in copies:
        copy.wait()


def kept_after(tick, common, added, kept):
    stashes = [
        (pltpu.HBM, (TICKS, CELLS, FCH)),
        (pltpu.HBM, (TICKS, CCELLS, CCH)),
        (pltpu.HBM, (6, CELLS, FCH)),
        (pltpu.HBM, (2, CCELLS, CCH)),
    ]
    earlier = () if tick == 0 else tuple(kept[:3]) if tick == 2 else tuple(kept)
    start = len(common) + len(added)
    return call(
        functools.partial(keep, tick),
        stashes,
        [SM, VM, VM, ANY, ANY] + [VM if tick == 3 else ANY] * len(added) + [ANY] * len(earlier),
        (
            pltpu.VMEM((CELLS, FCH), BF16),
            pltpu.VMEM((CCELLS, CCH), BF16),
            pltpu.VMEM((FCH, FCH), BF16),
            pltpu.VMEM((CCH, CCH), BF16),
            pltpu.VMEM((4, CELLS, FCH), BF16),
            pltpu.SemaphoreType.DMA((6,)),
        ),
        40_000_000,
        1_000_000,
        {start + i: i for i in range(len(earlier))},
    )(*common, *added, *earlier)


def tied(*values):
    return lax.optimization_barrier(values)


def on_device(
    fine_inflow,
    coarse_inflow,
    fine_entries,
    fine_pending,
    coarse_pending,
    fine_kernels,
    fine_mixing,
    fine_gains,
    fine_shifts,
    coarse_kernel,
    coarse_mixing,
    coarse_gains,
    coarse_shifts,
    descent_kernel,
    upsample_kernel,
):
    place = jnp.stack([lax.axis_index("segment"), lax.axis_index("dp") % 2]).astype(jnp.int32)
    inflow = fine_inflow.reshape(CELLS, FCH)
    cinflow = coarse_inflow.reshape(CCELLS, CCH)
    entries = fine_entries.reshape(TICKS - 1, CELLS, FCH)
    pending = fine_pending.reshape(6, CELLS, FCH)
    cpending = coarse_pending.reshape(2, CCELLS, CCH)
    kernels = fine_kernels.reshape(2, 3, 3 * FCH, FCH)
    ckernel = coarse_kernel.reshape(3, 3 * CCH, CCH)
    mixing = fine_mixing.reshape(FCH, FCH)
    cmixing = coarse_mixing.reshape(CCH, CCH)
    gains, shifts = fine_gains.reshape(2, FCH), fine_shifts.reshape(2, FCH)
    cgains, cshifts = coarse_gains.reshape(1, CCH), coarse_shifts.reshape(1, CCH)
    descent = descent_kernel.reshape(4 * FCH, CCH)
    upsampling = upsample_kernel.transpose(1, 2, 0, 3).reshape(4, CCH, FCH)

    fine_route = [(0, 1), (1, 2), (2, 3), (4, 5), (5, 6), (6, 7)]
    up_route = [(HALF - 1, HALF)]
    coarse_route = [(p, (p + 1) % (2 * HALF)) for p in range(2 * HALF)]
    to_decoder = [(p, p + HALF) for p in range(HALF)]
    to_encoder = [(p + HALF, p) for p in range(HALF)]
    cores = [(i, i ^ 1) for i in range(N_DP)]

    ftile, ctile = (CELLS, FCH), (CCELLS, CCH)
    fine_bf, coarse_bf = pltpu.VMEM(ftile, BF16), pltpu.VMEM(ctile, BF16)
    padded = pltpu.VMEM((CELLS + 2 * SIDE, 3 * FCH), BF16)
    vmem, hbm = pltpu.VMEM, pltpu.HBM
    kernel_kept = (vmem, (3, 3 * FCH, FCH))
    conv_flops = 2 * CELLS * 9 * FCH * FCH

    arrived = raised = carrived = kept = None
    for tick in range(TICKS):
        sending = tick < TICKS - 1
        if tick == 0:
            sources, specs = (inflow, pending, mixing, kernels), [SM, ANY, ANY, ANY, ANY]
            more = (pltpu.VMEM((4, CELLS, FCH), BF16), pltpu.SemaphoreType.DMA((6,)))
        else:
            sources = (arrived, raised, entries, upsampling, pending, mixing, kernel_one)
            specs = [SM, VM, VM, ANY, ANY, ANY, ANY, VM]
            more = (
                pltpu.VMEM((2, CELLS, 128), F32),
                pltpu.VMEM((4, CCH, FCH), BF16),
                pltpu.SemaphoreType.DMA((4,)),
            )
        h1, pay, *handed = call(
            functools.partial(fine_first, tick),
            [(vmem, ftile, F32), (vmem, (N_DP, 4, 128), F32)] + ([(hbm, (4, CELLS, FCH)), kernel_kept, kernel_kept] if tick == 0 else []),
            specs,
            (fine_bf, padded, fine_bf, pltpu.VMEM((FCH, FCH), BF16), pltpu.SemaphoreType.DMA((6,)), *more),
            conv_flops,
            1_000_000,
        )(place, *sources)

        if tick == 0:
            carrived = cinflow
            packed, kernel_one, kernel_two = handed
            pay, later = tied(pay, place)
            skips = lax.ppermute(packed, "segment", to_decoder)
        else:
            pay, carrived = tied(pay, carrived)
            later = place
        gathered = lax.all_to_all(pay, "dp", 0, 0, tiled=True)
        hc, mine, other = call(
            functools.partial(coarse_first, tick),
            [(vmem, ctile, F32), (vmem, (4, 128), F32), (vmem, (4, 128), F32)],
            [SM, VM if tick else ANY, ANY, ANY, ANY],
            (
                coarse_bf,
                pltpu.VMEM((3, CCELLS, 3 * CCH), BF16),
                pltpu.VMEM((CCH, CCH), BF16),
                pltpu.VMEM((3, 3 * CCH, CCH), BF16),
                pltpu.SemaphoreType.DMA((7,)),
                coarse_bf,
            ),
            2 * CCELLS * 9 * CCH * CCH,
            1_500_000,
        )(later, carrived, cpending if tick < 2 else cskips, cmixing, ckernel)
        theirs = lax.ppermute(other, "dp", cores)
        h2, pay2 = call(
            fine_second,
            [(vmem, ftile, F32), (vmem, (N_DP, 8, 128), F32)],
            [VM] * 7,
            (padded,),
            conv_flops,
            1_000_000,
        )(gathered, h1, gains, shifts, kernel_two, mine, theirs)
        if tick > 0:
            pay2, own, cown = tied(pay2, own, cown)
        gathered2 = lax.all_to_all(pay2, "dp", 0, 0, tiled=True)
        if tick == 0:
            cskips = lax.ppermute(tied(cpending, pay)[0], "segment", to_encoder)
            gathered2, skips = tied(gathered2, skips)
        else:
            added = ((pending,), (), (skips,))[tick - 1]
            kept = kept_after(tick - 1, (place, own, cown, mixing, cmixing), added, kept)
            gathered2, *kept = tied(gathered2, *kept)
            if tick == 1:
                gathered2, cskips = tied(gathered2, cskips)
            if tick == 2:
                fresh = lax.ppermute(kept[3], "segment", to_encoder)
        own, cown = call(
            functools.partial(finish, tick),
            [(vmem, ftile), (vmem, ctile)],
            [VM] * 7,
            (),
            1_000_000,
            1_000_000,
        )(gathered2, h2, hc, gains, shifts, cgains, cshifts)
        if sending:
            raised = lax.ppermute(cown, "segment", up_route)
            arrived = lax.ppermute(own, "segment", fine_route)
            (going,) = call(
                coarse_sent,
                [(vmem, ctile)],
                [SM, VM, VM, ANY],
                (
                    pltpu.VMEM((CELLS, 128), F32),
                    pltpu.VMEM((CCELLS, 4 * FCH), BF16),
                    pltpu.VMEM((4 * FCH, CCH), BF16),
                    pltpu.SemaphoreType.DMA,
                ),
                100_000_000,
                1_000_000,
            )(place, own, cown, descent)
            carrived = lax.ppermute(going, "segment", coarse_route)
    fstash, cstash, fback, cback = kept_after(
        TICKS - 1, (place, own, cown, mixing, cmixing), (fresh,), kept
    )
    return (
        fstash.reshape(1, TICKS, 1, SIDE, SIDE, FCH),
        cstash.reshape(1, TICKS, 1, CSIDE, CSIDE, CCH),
        fback.reshape(1, 6, 1, SIDE, SIDE, FCH),
        cback.reshape(1, 2, 1, CSIDE, CSIDE, CCH),
    )


def solution(mesh):
    placed = (
        P("segment", "dp", None, None, None),
        P("segment", "dp", None, None, None),
        P(None, "dp", None, None, None),
        P("segment", None, "dp", None, None, None),
        P("segment", None, "dp", None, None, None),
        P("segment", None, None, None, None, None),
        P("segment", None, None),
        P("segment", None, None),
        P("segment", None, None),
        P("segment", None, None, None, None),
        P("segment", None, None),
        P("segment", None),
        P("segment", None),
        P(),
        P(),
    )
    return jax.shard_map(
        on_device,
        mesh=mesh,
        in_specs=placed,
        out_specs=(P("segment", None, "dp", None, None, None),) * 4,
        check_vma=False,
    )
```

```python
import functools

import jax
import jax.numpy as jnp
from jax import lax
from jax.experimental import pallas as pl
from jax.experimental.pallas import tpu as pltpu
from jax.sharding import PartitionSpec as P

EPSILON = 1e-05
BF16 = jnp.bfloat16
F32 = jnp.float32
LIMIT = 24 * 1024 * 1024

SIDE, CSIDE = 16, 8
CELLS, CCELLS = SIDE * SIDE, CSIDE * CSIDE
FCH, CCH = 256, 512
N_DP = 32
HALF = 4
LAST = 2 * HALF - 1
TICKS = 4


def call(body, outs, in_specs, scratch=(), flops=0, moved=0, aliases=None):
    kernel = pl.pallas_call(
        body,
        out_shape=[space(*rest) if len(rest) == 2 else space(*rest, BF16) for space, *rest in outs],
        in_specs=in_specs,
        out_specs=[VM if space is pltpu.VMEM else ANY for space, *_ in outs],
        scratch_shapes=list(scratch),
        input_output_aliases=aliases or {},
        compiler_params=pltpu.CompilerParams(vmem_limit_bytes=LIMIT),
        cost_estimate=pl.CostEstimate(flops=flops, bytes_accessed=moved, transcendentals=0),
    )
    spaces = {id(VM): pltpu.VMEM, id(ANY): pltpu.HBM}

    def placed(spec, x):
        return pltpu.with_memory_space_constraint(x, spaces[id(spec)]) if id(spec) in spaces else x

    return lambda *args: kernel(*[placed(spec, arg) for spec, arg in zip(in_specs, args, strict=True)])


VM = pl.BlockSpec(memory_space=pltpu.VMEM)
SM = pl.BlockSpec(memory_space=pltpu.SMEM)
ANY = pl.BlockSpec(memory_space=pl.ANY)


def dot(a, b):
    return jnp.dot(a, b, preferred_element_type=F32)


def lanes(rows):
    return jnp.concatenate([rows[i : i + 1] for i in range(rows.shape[0])], axis=1)


def rows_of(line):
    return [line[:, i : i + 128] for i in range(0, line.shape[1], 128)]


def with_neighbours(x, width):
    count = x.shape[0]
    column = lax.broadcasted_iota(jnp.int32, x.shape, 0) & (width - 1)
    left = jnp.where(column == 0, 0.0, pltpu.roll(x, 1, 0))
    right = jnp.where(column == width - 1, 0.0, pltpu.roll(x, count - 1, 0))
    return left, x, right


class Streamed:
    def __init__(self, source, held, sems):
        self.held = held
        self.copies = [
            pltpu.make_async_copy(source.at[i], held.at[i], sems.at[i]) for i in range(held.shape[0])
        ]

    def start(self):
        for copy in self.copies:
            copy.start()
        return self

    def __getitem__(self, i):
        self.copies[i].wait()
        return self.held[i]


def fine_convolution(x, padded, kernel):
    edge = jnp.zeros((SIDE, 3 * FCH), BF16)
    padded[0:SIDE, :] = edge
    padded[SIDE + CELLS : 2 * SIDE + CELLS, :] = edge
    for i, piece in enumerate(with_neighbours(x, SIDE)):
        padded[SIDE : SIDE + CELLS, i * FCH : (i + 1) * FCH] = piece.astype(BF16)
    total = dot(padded[0:CELLS, :], kernel[0])
    total += dot(padded[SIDE : SIDE + CELLS, :], kernel[1])
    total += dot(padded[2 * SIDE : 2 * SIDE + CELLS, :], kernel[2])
    return total


def local_moments(h):
    mean = jnp.sum(h, axis=0, keepdims=True) * (1.0 / h.shape[0])
    away = h - mean
    return mean, jnp.sum(away * away, axis=0, keepdims=True)


def merged(pieces, cells_each):
    count = len(pieces)
    k = pieces[0].shape[0] // 2
    total = functools.reduce(jnp.add, pieces)
    mean = total * (1.0 / count)
    drift = functools.reduce(jnp.add, [jnp.square(piece - mean) for piece in pieces])
    spread = (total[k:] + cells_each * drift[:k]) * (1.0 / (count * cells_each))
    return lanes(mean[:k]), lanes(spread)


def activated(h, mean, spread, gain, shift):
    return jnp.maximum((h - mean) * lax.rsqrt(spread + EPSILON) * gain + shift, 0.0)


def fine_first(tick, *refs):
    if tick == 0:
        place, inflow, pending, mixing, kernels = refs[:5]
        refs = refs[5:]
    else:
        place, arrived, raised_in, entries, raising, pending, mixing, kernels = refs[:8]
        refs = refs[8:]
    h_ref, pay_ref = refs[:2]
    if tick == 0:
        parts, held, second = refs[2:6], refs[6], refs[7]
        x_ref, padded, skip_ref, mix_ref, sems, staged, pack_sems = refs[8:]
    else:
        x_ref, padded, skip_ref, mix_ref, sems, spread_ref, up_ref, up_sems = refs[2:]
    segment = place[0]
    kernel = Streamed(kernels.at[0], held, sems.at[pl.ds(0, 3)]) if tick == 0 else kernels
    skip = pltpu.make_async_copy(pending.at[tick], skip_ref, sems.at[3])
    mix = pltpu.make_async_copy(mixing, mix_ref, sems.at[4])

    if tick == 0:
        x = pltpu.make_async_copy(inflow, x_ref, sems.at[5])
        x.start()
    else:
        up = Streamed(raising, up_ref, up_sems)

        @pl.when(segment == HALF)
        def _():
            up.start()

        @pl.when(segment == 0)
        def _():
            pltpu.make_async_copy(entries.at[tick - 1], x_ref, sems.at[5]).start()

    @pl.when(segment >= HALF)
    def _():
        mix.start()
        skip.start()

    if tick == 0:
        kernel.start()
        onward = pltpu.make_async_copy(kernels.at[1], second, pack_sems.at[5])
        onward.start()
        loads = [pltpu.make_async_copy(pending.at[slot], staged.at[slot], pack_sems.at[slot]) for slot in range(4)]
        stores = [pltpu.make_async_copy(staged.at[slot], parts[slot], pack_sems.at[slot]) for slot in range(4)]

        @pl.when(segment < HALF)
        def _():
            for copy in loads:
                copy.start()

    if tick == 0:
        x.wait()
    else:

        @pl.when(segment == 0)
        def _():
            pltpu.make_async_copy(entries.at[tick - 1], x_ref, sems.at[5]).wait()

        @pl.when((segment != 0) & (segment != HALF))
        def _():
            x_ref[...] = arrived[...]

        @pl.when(segment == HALF)
        def _():
            for part in range(4):
                raised = dot(raised_in[...], up[part])
                for i in range(CSIDE):
                    start = (2 * i + part // 2) * SIDE + part % 2
                    for p in range(FCH // 128):
                        spread_ref[p, pl.ds(start, CSIDE, stride=2), :] = raised[
                            i * CSIDE : (i + 1) * CSIDE, p * 128 : (p + 1) * 128
                        ]
            for p in range(FCH // 128):
                x_ref[:, p * 128 : (p + 1) * 128] = spread_ref[p].astype(BF16)

    @pl.when(segment >= HALF)
    def _():
        skip.wait()
        mix.wait()
        x_ref[...] = (dot(x_ref[...], mix_ref[...]) + skip_ref[...].astype(F32)).astype(BF16)

    if tick == 0:

        @pl.when(segment < HALF)
        def _():
            for load, store in zip(loads, stores):
                load.wait()
                store.start()

    h = fine_convolution(x_ref[...].astype(F32), padded, kernel)
    h_ref[...] = h
    mean, spread = local_moments(h)
    pay = jnp.concatenate(rows_of(mean) + rows_of(spread), axis=0)
    pay_ref[...] = jnp.broadcast_to(pay[None], pay_ref.shape)
    if tick == 0:
        onward.wait()

        @pl.when(segment < HALF)
        def _():
            for store in stores:
                store.wait()


def coarse_first(tick, *refs):
    place, arrived, pending, mixing, kernels = refs[:5]
    h_ref, mine_ref, other_ref, x_ref, padded, mix_ref, held, sems, skip_ref = refs[5:]
    kernel = Streamed(kernels, held, sems.at[pl.ds(3, 3)])
    skips = [pltpu.make_async_copy(pending.at[tick % 2], skip_ref, sems.at[1])]
    segment = place[0]
    mix = pltpu.make_async_copy(mixing, mix_ref, sems.at[0])

    @pl.when(segment < HALF)
    def _():
        mix.start()
        for skip in skips:
            skip.start()

    if tick == 0:
        fetch = pltpu.make_async_copy(arrived, x_ref, sems.at[2])
        fetch.start()
    kernel.start()
    if tick == 0:
        fetch.wait()
    else:
        x_ref[...] = arrived[...]
    @pl.when(segment < HALF)
    def _():
        mix.wait()
        for skip in skips:
            skip.wait()
        x_ref[...] = (dot(x_ref[...], mix_ref[...]) + skip_ref[...].astype(F32)).astype(BF16)

    edge = jnp.zeros((CSIDE, CCH), F32)
    for i, piece in enumerate(with_neighbours(x_ref[...].astype(F32), CSIDE)):
        columns = slice(i * CCH, (i + 1) * CCH)
        padded[0, :, columns] = jnp.concatenate([edge, piece[: CCELLS - CSIDE]], axis=0).astype(BF16)
        padded[1, :, columns] = piece.astype(BF16)
        padded[2, :, columns] = jnp.concatenate([piece[CSIDE:], edge], axis=0).astype(BF16)
    h = dot(padded[0], kernel[0])
    h += dot(padded[1], kernel[1])
    h += dot(padded[2], kernel[2])
    h_ref[...] = h
    mean, spread = local_moments(h)
    mean, spread = rows_of(mean), rows_of(spread)
    first = jnp.concatenate(mean[:2] + spread[:2], axis=0)
    second = jnp.concatenate(mean[2:] + spread[2:], axis=0)
    is_first = place[1] == 0
    mine_ref[...] = jnp.where(is_first, first, second)
    other_ref[...] = jnp.where(is_first, second, first)


def fine_second(gathered, h_ref, gains, shifts, kernel, mine, theirs, out_ref, pay_ref, padded):
    mean, spread = merged([gathered[i] for i in range(N_DP)], float(CELLS))
    x = activated(h_ref[...], mean, spread, gains[0:1], shifts[0:1]).astype(BF16)
    h = fine_convolution(x.astype(F32), padded, kernel)
    out_ref[...] = h
    mean, spread = local_moments(h)
    a, b = mine[...], theirs[...]
    pair_mean = (a[:2] + b[:2]) * 0.5
    pair_spread = a[2:] + b[2:] + jnp.square(a[:2] - b[:2]) * (0.5 * CCELLS)
    pay = jnp.concatenate(rows_of(mean) + rows_of(spread) + [pair_mean, pair_spread], axis=0)
    pay_ref[...] = jnp.broadcast_to(pay[None], pay_ref.shape)


def finish(tick, gathered, h_ref, hc_ref, gains, shifts, cgains, cshifts, fine_ref, coarse_ref):
    mean, spread = merged([gathered[i, 0:4] for i in range(N_DP)], float(CELLS))
    fine_ref[...] = activated(h_ref[...], mean, spread, gains[1:2], shifts[1:2]).astype(BF16)
    mean0, spread0 = merged([gathered[i, 4:8] for i in range(0, N_DP, 2)], 2.0 * CCELLS)
    mean1, spread1 = merged([gathered[i, 4:8] for i in range(1, N_DP, 2)], 2.0 * CCELLS)
    mean = jnp.concatenate([mean0, mean1], axis=1)
    spread = jnp.concatenate([spread0, spread1], axis=1)
    coarse_ref[...] = activated(hc_ref[...], mean, spread, cgains[...], cshifts[...]).astype(BF16)


def coarse_sent(place, fine, coarse, descent, going, fine32, packed, down_ref, sem):
    segment = place[0]

    @pl.when(segment != HALF - 1)
    def _():
        going[...] = coarse[...]

    @pl.when(segment == HALF - 1)
    def _():
        fetch = pltpu.make_async_copy(descent, down_ref, sem)
        fetch.start()
        for p in range(FCH // 128):
            fine32[...] = fine[:, p * 128 : (p + 1) * 128].astype(F32)
            for a in range(2):
                for c in range(2):
                    taken = [fine32[pl.ds((2 * i + a) * SIDE + c, CSIDE, stride=2), :] for i in range(CSIDE)]
                    column = (2 * a + c) * FCH + p * 128
                    packed[:, column : column + 128] = jnp.concatenate(taken, axis=0).astype(BF16)
        fetch.wait()
        going[...] = dot(packed[...], down_ref[...]).astype(BF16)


def keep(tick, *refs):
    place, fine, coarse, got, mixing, cmixing = refs[:6]
    refs = refs[6:]
    if tick % 3 == 0:
        extra, refs = refs[0], refs[1:]
    fstash, cstash, fback, ctarget, term, cterm, mix_ref, cmix_ref, staged, sems = refs[(0, 4, 3, 4)[tick] :]
    segment = place[0]
    copies = [
        pltpu.make_async_copy(fine, fstash.at[tick], sems.at[0]),
        pltpu.make_async_copy(coarse, cstash.at[tick], sems.at[1]),
    ]
    for copy in copies:
        copy.start()
    if tick == 0:
        load = pltpu.make_async_copy(extra.at[4:6], staged.at[0:2], sems.at[2])
        load.start()

    @pl.when(segment < HALF)
    def _():
        fetch = pltpu.make_async_copy(mixing, mix_ref, sems.at[3])
        fetch.start()
        if tick == 3:
            ccopy = pltpu.make_async_copy(extra, ctarget, sems.at[5])
            ccopy.start()
        fetch.wait()
        term[...] = dot(fine[...], mix_ref[...]).astype(BF16)
        copy = pltpu.make_async_copy(term, fback.at[2 + tick], sems.at[4])
        copy.start()
        if tick == 3:
            ccopy.wait()
        copy.wait()

    @pl.when(segment >= HALF)
    def _():
        fetch = pltpu.make_async_copy(cmixing, cmix_ref, sems.at[3])
        fetch.start()
        received = pltpu.make_async_copy(got, fback.at[2 + tick], sems.at[4])
        received.start()
        fetch.wait()
        cterm[...] = dot(coarse[...], cmix_ref[...]).astype(BF16)
        copy = pltpu.make_async_copy(cterm, ctarget.at[tick % 2], sems.at[5])
        copy.start()
        received.wait()
        copy.wait()

    if tick == 0:
        load.wait()
        store = pltpu.make_async_copy(staged.at[0:2], fback.at[0:2], sems.at[2])
        store.start()
        store.wait()
    for copy in copies:
        copy.wait()


def kept_after(tick, common, added, kept):
    stashes = [
        (pltpu.HBM, (TICKS, CELLS, FCH)),
        (pltpu.HBM, (TICKS, CCELLS, CCH)),
        (pltpu.HBM, (6, CELLS, FCH)),
        (pltpu.HBM, (2, CCELLS, CCH)),
    ]
    earlier = () if tick == 0 else tuple(kept[:3]) if tick == 2 else tuple(kept)
    start = len(common) + len(added)
    return call(
        functools.partial(keep, tick),
        stashes,
        [SM, VM, VM, VM, ANY, ANY] + [VM if tick == 3 else ANY] * len(added) + [ANY] * len(earlier),
        (
            pltpu.VMEM((CELLS, FCH), BF16),
            pltpu.VMEM((CCELLS, CCH), BF16),
            pltpu.VMEM((FCH, FCH), BF16),
            pltpu.VMEM((CCH, CCH), BF16),
            pltpu.VMEM((2, CELLS, FCH), BF16),
            pltpu.SemaphoreType.DMA((6,)),
        ),
        40_000_000,
        1_000_000,
        {start + i: i for i in range(len(earlier))},
    )(*common, *added, *earlier)


def tied(*values):
    return lax.optimization_barrier(values)


def on_device(
    fine_inflow,
    coarse_inflow,
    fine_entries,
    fine_pending,
    coarse_pending,
    fine_kernels,
    fine_mixing,
    fine_gains,
    fine_shifts,
    coarse_kernel,
    coarse_mixing,
    coarse_gains,
    coarse_shifts,
    descent_kernel,
    upsample_kernel,
):
    place = jnp.stack([lax.axis_index("segment"), lax.axis_index("dp") % 2]).astype(jnp.int32)
    inflow = fine_inflow.reshape(CELLS, FCH)
    cinflow = coarse_inflow.reshape(CCELLS, CCH)
    entries = fine_entries.reshape(TICKS - 1, CELLS, FCH)
    pending = fine_pending.reshape(6, CELLS, FCH)
    cpending = coarse_pending.reshape(2, CCELLS, CCH)
    kernels = fine_kernels.reshape(2, 3, 3 * FCH, FCH)
    ckernel = coarse_kernel.reshape(3, 3 * CCH, CCH)
    mixing = fine_mixing.reshape(FCH, FCH)
    cmixing = coarse_mixing.reshape(CCH, CCH)
    gains, shifts = fine_gains.reshape(2, FCH), fine_shifts.reshape(2, FCH)
    cgains, cshifts = coarse_gains.reshape(1, CCH), coarse_shifts.reshape(1, CCH)
    descent = descent_kernel.reshape(4 * FCH, CCH)
    upsampling = upsample_kernel.transpose(1, 2, 0, 3).reshape(4, CCH, FCH)

    fine_route = [(0, 1), (1, 2), (2, 3), (4, 5), (5, 6), (6, 7)]
    up_route = [(HALF - 1, HALF)]
    coarse_route = [(p, (p + 1) % (2 * HALF)) for p in range(2 * HALF)]
    to_decoder = [(p, p + HALF) for p in range(HALF)]
    to_encoder = [(p + HALF, p) for p in range(HALF)]
    cores = [(i, i ^ 1) for i in range(N_DP)]

    ftile, ctile = (CELLS, FCH), (CCELLS, CCH)
    fine_bf, coarse_bf = pltpu.VMEM(ftile, BF16), pltpu.VMEM(ctile, BF16)
    padded = pltpu.VMEM((CELLS + 2 * SIDE, 3 * FCH), BF16)
    vmem, hbm = pltpu.VMEM, pltpu.HBM
    kernel_kept = (vmem, (3, 3 * FCH, FCH))
    conv_flops = 2 * CELLS * 9 * FCH * FCH

    arrived = raised = carrived = kept = None
    for tick in range(TICKS):
        sending = tick < TICKS - 1
        if tick == 0:
            sources, specs = (inflow, pending, mixing, kernels), [SM, ANY, ANY, ANY, ANY]
            more = (pltpu.VMEM((4, CELLS, FCH), BF16), pltpu.SemaphoreType.DMA((6,)))
        else:
            sources = (arrived, raised, entries, upsampling, pending, mixing, kernel_one)
            specs = [SM, VM, VM, ANY, ANY, ANY, ANY, VM]
            more = (
                pltpu.VMEM((2, CELLS, 128), F32),
                pltpu.VMEM((4, CCH, FCH), BF16),
                pltpu.SemaphoreType.DMA((4,)),
            )
        h1, pay, *handed = call(
            functools.partial(fine_first, tick),
            [(vmem, ftile, F32), (vmem, (N_DP, 4, 128), F32)] + ([(hbm, ftile)] * 4 + [kernel_kept, kernel_kept] if tick == 0 else []),
            specs,
            (fine_bf, padded, fine_bf, pltpu.VMEM((FCH, FCH), BF16), pltpu.SemaphoreType.DMA((6,)), *more),
            conv_flops,
            1_000_000,
        )(place, *sources)

        if tick == 0:
            carrived = cinflow
            *parts, kernel_one, kernel_two = handed
            pay, later = tied(pay, place)
        else:
            pay, carrived = tied(pay, carrived)
            later = place
        gathered = lax.all_to_all(pay, "dp", 0, 0, tiled=True)
        hc, mine, other = call(
            functools.partial(coarse_first, tick),
            [(vmem, ctile, F32), (vmem, (4, 128), F32), (vmem, (4, 128), F32)],
            [SM, VM if tick else ANY, ANY, ANY, ANY],
            (
                coarse_bf,
                pltpu.VMEM((3, CCELLS, 3 * CCH), BF16),
                pltpu.VMEM((CCH, CCH), BF16),
                pltpu.VMEM((3, 3 * CCH, CCH), BF16),
                pltpu.SemaphoreType.DMA((7,)),
                coarse_bf,
            ),
            2 * CCELLS * 9 * CCH * CCH,
            1_500_000,
        )(later, carrived, cpending if tick < 2 else cskips, cmixing, ckernel)
        theirs = lax.ppermute(other, "dp", cores)
        h2, pay2 = call(
            fine_second,
            [(vmem, ftile, F32), (vmem, (N_DP, 8, 128), F32)],
            [VM] * 7,
            (padded,),
            conv_flops,
            1_000_000,
        )(gathered, h1, gains, shifts, kernel_two, mine, theirs)
        if tick > 0:
            pay2, own, cown = tied(pay2, own, cown)
        pay2, skip = tied(pay2, parts[tick])
        gathered2 = lax.all_to_all(pay2, "dp", 0, 0, tiled=True)
        came = lax.ppermute(skip, "segment", to_decoder)
        if tick == 0:
            cskips = lax.ppermute(tied(cpending, pay2)[0], "segment", to_encoder)
            gathered2, cskips = tied(gathered2, cskips)
        else:
            added = (pending,) if tick == 1 else ()
            kept = kept_after(tick - 1, (place, own, cown, got, mixing, cmixing), added, kept)
            gathered2, *kept = tied(gathered2, *kept)
            if tick == 2:
                fresh = lax.ppermute(kept[3], "segment", to_encoder)
        gathered2, got = tied(gathered2, came)
        own, cown = call(
            functools.partial(finish, tick),
            [(vmem, ftile), (vmem, ctile)],
            [VM] * 7,
            (),
            1_000_000,
            1_000_000,
        )(gathered2, h2, hc, gains, shifts, cgains, cshifts)
        if sending:
            raised = lax.ppermute(cown, "segment", up_route)
            arrived = lax.ppermute(own, "segment", fine_route)
            (going,) = call(
                coarse_sent,
                [(vmem, ctile)],
                [SM, VM, VM, ANY],
                (
                    pltpu.VMEM((CELLS, 128), F32),
                    pltpu.VMEM((CCELLS, 4 * FCH), BF16),
                    pltpu.VMEM((4 * FCH, CCH), BF16),
                    pltpu.SemaphoreType.DMA,
                ),
                100_000_000,
                1_000_000,
            )(place, own, cown, descent)
            carrived = lax.ppermute(going, "segment", coarse_route)
    fstash, cstash, fback, cback = kept_after(
        TICKS - 1, (place, own, cown, got, mixing, cmixing), (fresh,), kept
    )
    return (
        fstash.reshape(1, TICKS, 1, SIDE, SIDE, FCH),
        cstash.reshape(1, TICKS, 1, CSIDE, CSIDE, CCH),
        fback.reshape(1, 6, 1, SIDE, SIDE, FCH),
        cback.reshape(1, 2, 1, CSIDE, CSIDE, CCH),
    )


def solution(mesh):
    placed = (
        P("segment", "dp", None, None, None),
        P("segment", "dp", None, None, None),
        P(None, "dp", None, None, None),
        P("segment", None, "dp", None, None, None),
        P("segment", None, "dp", None, None, None),
        P("segment", None, None, None, None, None),
        P("segment", None, None),
        P("segment", None, None),
        P("segment", None, None),
        P("segment", None, None, None, None),
        P("segment", None, None),
        P("segment", None),
        P("segment", None),
        P(),
        P(),
    )
    return jax.shard_map(
        on_device,
        mesh=mesh,
        in_specs=placed,
        out_specs=(P("segment", None, "dp", None, None, None),) * 4,
        check_vma=False,
    )
```

```python
import functools

import jax
import jax.numpy as jnp
from jax import lax
from jax.experimental import pallas as pl
from jax.experimental.pallas import tpu as pltpu
from jax.sharding import PartitionSpec as P

EPSILON = 1e-05
BF16 = jnp.bfloat16
F32 = jnp.float32
LIMIT = 24 * 1024 * 1024

SIDE, CSIDE = 16, 8
CELLS, CCELLS = SIDE * SIDE, CSIDE * CSIDE
FCH, CCH = 256, 512
N_DP = 32
HALF = 4
LAST = 2 * HALF - 1
TICKS = 4


def call(body, outs, in_specs, scratch=(), flops=0, moved=0, aliases=None):
    kernel = pl.pallas_call(
        body,
        out_shape=[space(*rest) if len(rest) == 2 else space(*rest, BF16) for space, *rest in outs],
        in_specs=in_specs,
        out_specs=[VM if space is pltpu.VMEM else ANY for space, *_ in outs],
        scratch_shapes=list(scratch),
        input_output_aliases=aliases or {},
        compiler_params=pltpu.CompilerParams(vmem_limit_bytes=LIMIT),
        cost_estimate=pl.CostEstimate(flops=flops, bytes_accessed=moved, transcendentals=0),
    )
    spaces = {id(VM): pltpu.VMEM, id(ANY): pltpu.HBM}

    def placed(spec, x):
        return pltpu.with_memory_space_constraint(x, spaces[id(spec)]) if id(spec) in spaces else x

    return lambda *args: kernel(*[placed(spec, arg) for spec, arg in zip(in_specs, args, strict=True)])


VM = pl.BlockSpec(memory_space=pltpu.VMEM)
SM = pl.BlockSpec(memory_space=pltpu.SMEM)
ANY = pl.BlockSpec(memory_space=pl.ANY)


def dot(a, b):
    return jnp.dot(a, b, preferred_element_type=F32)


def lanes(rows):
    return jnp.concatenate([rows[i : i + 1] for i in range(rows.shape[0])], axis=1)


def rows_of(line):
    return [line[:, i : i + 128] for i in range(0, line.shape[1], 128)]


def with_neighbours(x, width):
    count = x.shape[0]
    column = lax.broadcasted_iota(jnp.int32, x.shape, 0) & (width - 1)
    left = jnp.where(column == 0, 0.0, pltpu.roll(x, 1, 0))
    right = jnp.where(column == width - 1, 0.0, pltpu.roll(x, count - 1, 0))
    return left, x, right


class Streamed:
    def __init__(self, source, held, sems):
        self.held = held
        self.copies = [
            pltpu.make_async_copy(source.at[i], held.at[i], sems.at[i]) for i in range(held.shape[0])
        ]

    def start(self):
        for copy in self.copies:
            copy.start()
        return self

    def __getitem__(self, i):
        self.copies[i].wait()
        return self.held[i]


def fine_convolution(x, padded, kernel):
    edge = jnp.zeros((SIDE, 3 * FCH), BF16)
    padded[0:SIDE, :] = edge
    padded[SIDE + CELLS : 2 * SIDE + CELLS, :] = edge
    for i, piece in enumerate(with_neighbours(x, SIDE)):
        padded[SIDE : SIDE + CELLS, i * FCH : (i + 1) * FCH] = piece.astype(BF16)
    total = dot(padded[0:CELLS, :], kernel[0])
    total += dot(padded[SIDE : SIDE + CELLS, :], kernel[1])
    total += dot(padded[2 * SIDE : 2 * SIDE + CELLS, :], kernel[2])
    return total


def local_moments(h):
    mean = jnp.sum(h, axis=0, keepdims=True) * (1.0 / h.shape[0])
    away = h - mean
    return mean, jnp.sum(away * away, axis=0, keepdims=True)


def merged(pieces, cells_each):
    count = len(pieces)
    k = pieces[0].shape[0] // 2
    total = functools.reduce(jnp.add, pieces)
    mean = total * (1.0 / count)
    drift = functools.reduce(jnp.add, [jnp.square(piece - mean) for piece in pieces])
    spread = (total[k:] + cells_each * drift[:k]) * (1.0 / (count * cells_each))
    return lanes(mean[:k]), lanes(spread)


def activated(h, mean, spread, gain, shift):
    return jnp.maximum((h - mean) * lax.rsqrt(spread + EPSILON) * gain + shift, 0.0)


def fine_first(tick, *refs):
    if tick == 0:
        place, inflow, pending, mixing, kernels = refs[:5]
        refs = refs[5:]
    else:
        place, arrived, raised_in, entries, raising, pending, mixing, kernels = refs[:8]
        refs = refs[8:]
    h_ref, pay_ref = refs[:2]
    if tick == 0:
        packed, held, second, mix_ref = refs[2:6]
        x_ref, padded, skip_ref, sems, staged, pack_sems = refs[6:]
    else:
        x_ref, padded, skip_ref, sems, spread_ref, up_ref, up_sems = refs[2:]
        mix_ref = mixing
    segment = place[0]
    kernel = Streamed(kernels.at[0], held, sems.at[pl.ds(0, 3)]) if tick == 0 else kernels
    skip = pltpu.make_async_copy(pending.at[tick], skip_ref, sems.at[3])

    if tick == 0:
        mix = pltpu.make_async_copy(mixing, mix_ref, sems.at[4])
        mix.start()
        x = pltpu.make_async_copy(inflow, x_ref, sems.at[5])
        x.start()
    else:
        up = Streamed(raising, up_ref, up_sems)

        @pl.when(segment == HALF)
        def _():
            up.start()

        @pl.when(segment == 0)
        def _():
            pltpu.make_async_copy(entries.at[tick - 1], x_ref, sems.at[5]).start()

    @pl.when(segment >= HALF)
    def _():
        skip.start()

    if tick == 0:
        kernel.start()
        onward = pltpu.make_async_copy(kernels.at[1], second, pack_sems.at[5])
        onward.start()
        loads = [pltpu.make_async_copy(pending.at[slot], staged.at[slot], pack_sems.at[slot]) for slot in range(4)]
        store = pltpu.make_async_copy(staged, packed, pack_sems.at[4])

        @pl.when(segment < HALF)
        def _():
            for copy in loads:
                copy.start()

    if tick == 0:
        x.wait()
    else:

        @pl.when(segment == 0)
        def _():
            pltpu.make_async_copy(entries.at[tick - 1], x_ref, sems.at[5]).wait()

        @pl.when((segment != 0) & (segment != HALF))
        def _():
            x_ref[...] = arrived[...]

        @pl.when(segment == HALF)
        def _():
            for part in range(4):
                raised = dot(raised_in[...], up[part])
                for i in range(CSIDE):
                    start = (2 * i + part // 2) * SIDE + part % 2
                    for p in range(FCH // 128):
                        spread_ref[p, pl.ds(start, CSIDE, stride=2), :] = raised[
                            i * CSIDE : (i + 1) * CSIDE, p * 128 : (p + 1) * 128
                        ]
            for p in range(FCH // 128):
                x_ref[:, p * 128 : (p + 1) * 128] = spread_ref[p].astype(BF16)

    if tick == 0:
        mix.wait()

    @pl.when(segment >= HALF)
    def _():
        skip.wait()
        x_ref[...] = (dot(x_ref[...], mix_ref[...]) + skip_ref[...].astype(F32)).astype(BF16)

    if tick == 0:

        @pl.when(segment < HALF)
        def _():
            for copy in loads:
                copy.wait()
            store.start()

    h = fine_convolution(x_ref[...].astype(F32), padded, kernel)
    h_ref[...] = h
    mean, spread = local_moments(h)
    pay = jnp.concatenate(rows_of(mean) + rows_of(spread), axis=0)
    pay_ref[...] = jnp.broadcast_to(pay[None], pay_ref.shape)
    if tick == 0:
        onward.wait()

        @pl.when(segment < HALF)
        def _():
            store.wait()


def coarse_first(tick, *refs):
    place, arrived, pending, mixing, kernels = refs[:5]
    h_ref, mine_ref, other_ref, x_ref, padded, mix_ref, held, sems, skip_ref = refs[5:]
    kernel = Streamed(kernels, held, sems.at[pl.ds(3, 3)])
    skips = [pltpu.make_async_copy(pending.at[tick % 2], skip_ref, sems.at[1])]
    segment = place[0]
    mix = pltpu.make_async_copy(mixing, mix_ref, sems.at[0])

    @pl.when(segment < HALF)
    def _():
        mix.start()
        for skip in skips:
            skip.start()

    if tick == 0:
        fetch = pltpu.make_async_copy(arrived, x_ref, sems.at[2])
        fetch.start()
    kernel.start()
    if tick == 0:
        fetch.wait()
    else:
        x_ref[...] = arrived[...]
    @pl.when(segment < HALF)
    def _():
        mix.wait()
        for skip in skips:
            skip.wait()
        x_ref[...] = (dot(x_ref[...], mix_ref[...]) + skip_ref[...].astype(F32)).astype(BF16)

    edge = jnp.zeros((CSIDE, CCH), F32)
    for i, piece in enumerate(with_neighbours(x_ref[...].astype(F32), CSIDE)):
        columns = slice(i * CCH, (i + 1) * CCH)
        padded[0, :, columns] = jnp.concatenate([edge, piece[: CCELLS - CSIDE]], axis=0).astype(BF16)
        padded[1, :, columns] = piece.astype(BF16)
        padded[2, :, columns] = jnp.concatenate([piece[CSIDE:], edge], axis=0).astype(BF16)
    h = dot(padded[0], kernel[0])
    h += dot(padded[1], kernel[1])
    h += dot(padded[2], kernel[2])
    h_ref[...] = h
    mean, spread = local_moments(h)
    mean, spread = rows_of(mean), rows_of(spread)
    first = jnp.concatenate(mean[:2] + spread[:2], axis=0)
    second = jnp.concatenate(mean[2:] + spread[2:], axis=0)
    is_first = place[1] == 0
    mine_ref[...] = jnp.where(is_first, first, second)
    other_ref[...] = jnp.where(is_first, second, first)


def fine_second(gathered, h_ref, gains, shifts, kernel, mine, theirs, out_ref, pay_ref, padded):
    mean, spread = merged([gathered[i] for i in range(N_DP)], float(CELLS))
    x = activated(h_ref[...], mean, spread, gains[0:1], shifts[0:1]).astype(BF16)
    h = fine_convolution(x.astype(F32), padded, kernel)
    out_ref[...] = h
    mean, spread = local_moments(h)
    a, b = mine[...], theirs[...]
    pair_mean = (a[:2] + b[:2]) * 0.5
    pair_spread = a[2:] + b[2:] + jnp.square(a[:2] - b[:2]) * (0.5 * CCELLS)
    pay = jnp.concatenate(rows_of(mean) + rows_of(spread) + [pair_mean, pair_spread], axis=0)
    pay_ref[...] = jnp.broadcast_to(pay[None], pay_ref.shape)


def finish(tick, gathered, h_ref, hc_ref, gains, shifts, cgains, cshifts, fine_ref, coarse_ref):
    mean, spread = merged([gathered[i, 0:4] for i in range(N_DP)], float(CELLS))
    fine_ref[...] = activated(h_ref[...], mean, spread, gains[1:2], shifts[1:2]).astype(BF16)
    mean0, spread0 = merged([gathered[i, 4:8] for i in range(0, N_DP, 2)], 2.0 * CCELLS)
    mean1, spread1 = merged([gathered[i, 4:8] for i in range(1, N_DP, 2)], 2.0 * CCELLS)
    mean = jnp.concatenate([mean0, mean1], axis=1)
    spread = jnp.concatenate([spread0, spread1], axis=1)
    coarse_ref[...] = activated(hc_ref[...], mean, spread, cgains[...], cshifts[...]).astype(BF16)


def coarse_sent(place, fine, coarse, descent, going, fine32, packed, down_ref, sem):
    segment = place[0]

    @pl.when(segment != HALF - 1)
    def _():
        going[...] = coarse[...]

    @pl.when(segment == HALF - 1)
    def _():
        fetch = pltpu.make_async_copy(descent, down_ref, sem)
        fetch.start()
        for p in range(FCH // 128):
            fine32[...] = fine[:, p * 128 : (p + 1) * 128].astype(F32)
            for a in range(2):
                for c in range(2):
                    taken = [fine32[pl.ds((2 * i + a) * SIDE + c, CSIDE, stride=2), :] for i in range(CSIDE)]
                    column = (2 * a + c) * FCH + p * 128
                    packed[:, column : column + 128] = jnp.concatenate(taken, axis=0).astype(BF16)
        fetch.wait()
        going[...] = dot(packed[...], down_ref[...]).astype(BF16)


def keep(tick, *refs):
    place, fine, coarse, mixing, cmixing = refs[:5]
    refs = refs[5:]
    if tick in (0, 2):
        extra, refs = refs[0], refs[1:]
    fstash, cstash, fback, ctarget, term, cterm, mix_ref, cmix_ref, staged, sems = refs[(0, 4, 3, 4)[tick] :]
    segment = place[0]
    copies = [
        pltpu.make_async_copy(fine, fstash.at[tick], sems.at[0]),
        pltpu.make_async_copy(coarse, cstash.at[tick], sems.at[1]),
    ]
    for copy in copies:
        copy.start()
    if tick == 0:
        load = pltpu.make_async_copy(extra.at[4:6], staged.at[0:2], sems.at[2])
        load.start()

    @pl.when(segment < HALF)
    def _():
        fetch = pltpu.make_async_copy(mixing, mix_ref, sems.at[3])
        fetch.start()
        fetch.wait()
        term[...] = dot(fine[...], mix_ref[...]).astype(BF16)
        copy = pltpu.make_async_copy(term, fback.at[2 + tick], sems.at[4])
        copy.start()
        copy.wait()

    @pl.when(segment >= HALF)
    def _():
        fetch = pltpu.make_async_copy(cmixing, cmix_ref, sems.at[3])
        fetch.start()
        if tick == 2:
            received = pltpu.make_async_copy(extra, staged, sems.at[4])
            received.start()
        fetch.wait()
        cterm[...] = dot(coarse[...], cmix_ref[...]).astype(BF16)
        copy = pltpu.make_async_copy(cterm, ctarget.at[tick % 2], sems.at[5])
        copy.start()
        if tick == 2:
            received.wait()
            stored = pltpu.make_async_copy(staged, fback.at[2:6], sems.at[4])
            stored.start()
            stored.wait()
        copy.wait()

    if tick == 0:
        load.wait()
        store = pltpu.make_async_copy(staged.at[0:2], fback.at[0:2], sems.at[2])
        store.start()
        store.wait()
    for copy in copies:
        copy.wait()


def settle(place, received, _, target, sem):
    @pl.when(place[0] < HALF)
    def _():
        copy = pltpu.make_async_copy(received, target, sem)
        copy.start()
        copy.wait()


def kept_after(tick, common, added, kept):
    stashes = [
        (pltpu.HBM, (TICKS, CELLS, FCH)),
        (pltpu.HBM, (TICKS, CCELLS, CCH)),
        (pltpu.HBM, (6, CELLS, FCH)),
        (pltpu.HBM, (2, CCELLS, CCH)),
    ]
    earlier = () if tick == 0 else tuple(kept[:3]) if tick == 2 else tuple(kept)
    start = len(common) + len(added)
    return call(
        functools.partial(keep, tick),
        stashes,
        [SM, VM, VM, ANY, ANY] + [ANY] * (len(added) + len(earlier)),
        (
            pltpu.VMEM((CELLS, FCH), BF16),
            pltpu.VMEM((CCELLS, CCH), BF16),
            pltpu.VMEM((FCH, FCH), BF16),
            pltpu.VMEM((CCH, CCH), BF16),
            pltpu.VMEM((4, CELLS, FCH), BF16),
            pltpu.SemaphoreType.DMA((6,)),
        ),
        40_000_000,
        1_000_000,
        {start + i: i for i in range(len(earlier))},
    )(*common, *added, *earlier)


def tied(*values):
    return lax.optimization_barrier(values)


def on_device(
    fine_inflow,
    coarse_inflow,
    fine_entries,
    fine_pending,
    coarse_pending,
    fine_kernels,
    fine_mixing,
    fine_gains,
    fine_shifts,
    coarse_kernel,
    coarse_mixing,
    coarse_gains,
    coarse_shifts,
    descent_kernel,
    upsample_kernel,
):
    place = jnp.stack([lax.axis_index("segment"), lax.axis_index("dp") % 2]).astype(jnp.int32)
    inflow = fine_inflow.reshape(CELLS, FCH)
    cinflow = coarse_inflow.reshape(CCELLS, CCH)
    entries = fine_entries.reshape(TICKS - 1, CELLS, FCH)
    pending = fine_pending.reshape(6, CELLS, FCH)
    cpending = coarse_pending.reshape(2, CCELLS, CCH)
    kernels = fine_kernels.reshape(2, 3, 3 * FCH, FCH)
    ckernel = coarse_kernel.reshape(3, 3 * CCH, CCH)
    mixing = fine_mixing.reshape(FCH, FCH)
    cmixing = coarse_mixing.reshape(CCH, CCH)
    gains, shifts = fine_gains.reshape(2, FCH), fine_shifts.reshape(2, FCH)
    cgains, cshifts = coarse_gains.reshape(1, CCH), coarse_shifts.reshape(1, CCH)
    descent = descent_kernel.reshape(4 * FCH, CCH)
    upsampling = upsample_kernel.transpose(1, 2, 0, 3).reshape(4, CCH, FCH)

    fine_route = [(0, 1), (1, 2), (2, 3), (4, 5), (5, 6), (6, 7)]
    up_route = [(HALF - 1, HALF)]
    coarse_route = [(p, (p + 1) % (2 * HALF)) for p in range(2 * HALF)]
    to_decoder = [(p, p + HALF) for p in range(HALF)]
    to_encoder = [(p + HALF, p) for p in range(HALF)]
    cores = [(i, i ^ 1) for i in range(N_DP)]

    ftile, ctile = (CELLS, FCH), (CCELLS, CCH)
    fine_bf, coarse_bf = pltpu.VMEM(ftile, BF16), pltpu.VMEM(ctile, BF16)
    padded = pltpu.VMEM((CELLS + 2 * SIDE, 3 * FCH), BF16)
    vmem, hbm = pltpu.VMEM, pltpu.HBM
    kernel_kept = (vmem, (3, 3 * FCH, FCH))
    conv_flops = 2 * CELLS * 9 * FCH * FCH

    arrived = raised = carrived = kept = None
    for tick in range(TICKS):
        sending = tick < TICKS - 1
        if tick == 0:
            sources, specs = (inflow, pending, mixing, kernels), [SM, ANY, ANY, ANY, ANY]
            more = (pltpu.VMEM((4, CELLS, FCH), BF16), pltpu.SemaphoreType.DMA((6,)))
        else:
            sources = (arrived, raised, entries, upsampling, pending, near_mixing, kernel_one)
            specs = [SM, VM, VM, ANY, ANY, ANY, VM, VM]
            more = (
                pltpu.VMEM((2, CELLS, 128), F32),
                pltpu.VMEM((4, CCH, FCH), BF16),
                pltpu.SemaphoreType.DMA((4,)),
            )
        h1, pay, *handed = call(
            functools.partial(fine_first, tick),
            [(vmem, ftile, F32), (vmem, (N_DP, 4, 128), F32)] + ([(hbm, (4, CELLS, FCH)), kernel_kept, kernel_kept, (vmem, (FCH, FCH))] if tick == 0 else []),
            specs,
            (fine_bf, padded, fine_bf, pltpu.SemaphoreType.DMA((6,)), *more),
            conv_flops,
            1_000_000,
        )(place, *sources)

        if tick == 0:
            carrived = cinflow
            packed, kernel_one, kernel_two, near_mixing = handed
            pay, later = tied(pay, place)
            skips = lax.ppermute(packed, "segment", to_decoder)
        else:
            pay, carrived = tied(pay, carrived)
            later = place
        gathered = lax.all_to_all(pay, "dp", 0, 0, tiled=True)
        hc, mine, other = call(
            functools.partial(coarse_first, tick),
            [(vmem, ctile, F32), (vmem, (4, 128), F32), (vmem, (4, 128), F32)],
            [SM, VM if tick else ANY, ANY, ANY, ANY],
            (
                coarse_bf,
                pltpu.VMEM((3, CCELLS, 3 * CCH), BF16),
                pltpu.VMEM((CCH, CCH), BF16),
                pltpu.VMEM((3, 3 * CCH, CCH), BF16),
                pltpu.SemaphoreType.DMA((7,)),
                coarse_bf,
            ),
            2 * CCELLS * 9 * CCH * CCH,
            1_500_000,
        )(later, carrived, cpending if tick < 2 else cskips, cmixing, ckernel)
        theirs = lax.ppermute(other, "dp", cores)
        if tick == 2:
            gathered, skips = tied(gathered, skips)
        h2, pay2 = call(
            fine_second,
            [(vmem, ftile, F32), (vmem, (N_DP, 8, 128), F32)],
            [VM] * 7,
            (padded,),
            conv_flops,
            1_000_000,
        )(gathered, h1, gains, shifts, kernel_two, mine, theirs)
        if tick > 0:
            pay2, own, cown = tied(pay2, own, cown)
        gathered2 = lax.all_to_all(pay2, "dp", 0, 0, tiled=True)
        if tick == 0:
            cskips = lax.ppermute(tied(cpending, pay2)[0], "segment", to_encoder)
            gathered2, cskips = tied(gathered2, cskips)
        else:
            added = ((pending,), (), (skips,))[tick - 1]
            kept = kept_after(tick - 1, (place, own, cown, mixing, cmixing), added, kept)
            gathered2, *kept = tied(gathered2, *kept)
            if tick == 2:
                fresh = lax.ppermute(kept[3], "segment", to_encoder)
        own, cown = call(
            functools.partial(finish, tick),
            [(vmem, ftile), (vmem, ctile)],
            [VM] * 7,
            (),
            1_000_000,
            1_000_000,
        )(gathered2, h2, hc, gains, shifts, cgains, cshifts)
        if sending:
            raised = lax.ppermute(cown, "segment", up_route)
            arrived = lax.ppermute(own, "segment", fine_route)
            (going,) = call(
                coarse_sent,
                [(vmem, ctile)],
                [SM, VM, VM, ANY],
                (
                    pltpu.VMEM((CELLS, 128), F32),
                    pltpu.VMEM((CCELLS, 4 * FCH), BF16),
                    pltpu.VMEM((4 * FCH, CCH), BF16),
                    pltpu.SemaphoreType.DMA,
                ),
                100_000_000,
                1_000_000,
            )(place, own, cown, descent)
            carrived = lax.ppermute(going, "segment", coarse_route)
    fstash, cstash, fback, cback = kept_after(
        TICKS - 1, (place, own, cown, mixing, cmixing), (), kept
    )
    (cback,) = call(
        settle,
        [(hbm, (2, CCELLS, CCH))],
        [SM, VM, ANY],
        (pltpu.SemaphoreType.DMA,),
        0,
        300_000,
        {2: 0},
    )(place, fresh, cback)
    return (
        fstash.reshape(1, TICKS, 1, SIDE, SIDE, FCH),
        cstash.reshape(1, TICKS, 1, CSIDE, CSIDE, CCH),
        fback.reshape(1, 6, 1, SIDE, SIDE, FCH),
        cback.reshape(1, 2, 1, CSIDE, CSIDE, CCH),
    )


def solution(mesh):
    placed = (
        P("segment", "dp", None, None, None),
        P("segment", "dp", None, None, None),
        P(None, "dp", None, None, None),
        P("segment", None, "dp", None, None, None),
        P("segment", None, "dp", None, None, None),
        P("segment", None, None, None, None, None),
        P("segment", None, None),
        P("segment", None, None),
        P("segment", None, None),
        P("segment", None, None, None, None),
        P("segment", None, None),
        P("segment", None),
        P("segment", None),
        P(),
        P(),
    )
    return jax.shard_map(
        on_device,
        mesh=mesh,
        in_specs=placed,
        out_specs=(P("segment", None, "dp", None, None, None),) * 4,
        check_vma=False,
    )
```

```python
import functools

import jax
import jax.numpy as jnp
from jax import lax
from jax.experimental import pallas as pl
from jax.experimental.pallas import tpu as pltpu
from jax.sharding import PartitionSpec as P

EPSILON = 1e-05
BF16 = jnp.bfloat16
F32 = jnp.float32
LIMIT = 24 * 1024 * 1024

SIDE, CSIDE = 16, 8
CELLS, CCELLS = SIDE * SIDE, CSIDE * CSIDE
FCH, CCH = 256, 512
N_DP = 32
HALF = 4
LAST = 2 * HALF - 1
TICKS = 4


def call(body, outs, in_specs, scratch=(), flops=0, moved=0, aliases=None):
    kernel = pl.pallas_call(
        body,
        out_shape=[space(*rest) if len(rest) == 2 else space(*rest, BF16) for space, *rest in outs],
        in_specs=in_specs,
        out_specs=[VM if space is pltpu.VMEM else ANY for space, *_ in outs],
        scratch_shapes=list(scratch),
        input_output_aliases=aliases or {},
        compiler_params=pltpu.CompilerParams(vmem_limit_bytes=LIMIT),
        cost_estimate=pl.CostEstimate(flops=flops, bytes_accessed=moved, transcendentals=0),
    )
    spaces = {id(VM): pltpu.VMEM, id(ANY): pltpu.HBM}

    def placed(spec, x):
        return pltpu.with_memory_space_constraint(x, spaces[id(spec)]) if id(spec) in spaces else x

    return lambda *args: kernel(*[placed(spec, arg) for spec, arg in zip(in_specs, args, strict=True)])


VM = pl.BlockSpec(memory_space=pltpu.VMEM)
SM = pl.BlockSpec(memory_space=pltpu.SMEM)
ANY = pl.BlockSpec(memory_space=pl.ANY)


def dot(a, b):
    return jnp.dot(a, b, preferred_element_type=F32)


def lanes(rows):
    return jnp.concatenate([rows[i : i + 1] for i in range(rows.shape[0])], axis=1)


def rows_of(line):
    return [line[:, i : i + 128] for i in range(0, line.shape[1], 128)]


def with_neighbours(x, width):
    count = x.shape[0]
    column = lax.broadcasted_iota(jnp.int32, x.shape, 0) & (width - 1)
    left = jnp.where(column == 0, 0.0, pltpu.roll(x, 1, 0))
    right = jnp.where(column == width - 1, 0.0, pltpu.roll(x, count - 1, 0))
    return left, x, right


class Streamed:
    def __init__(self, source, held, sems):
        self.held = held
        self.copies = [
            pltpu.make_async_copy(source.at[i], held.at[i], sems.at[i]) for i in range(held.shape[0])
        ]

    def start(self):
        for copy in self.copies:
            copy.start()
        return self

    def __getitem__(self, i):
        self.copies[i].wait()
        return self.held[i]


def fine_convolution(x, padded, kernel):
    edge = jnp.zeros((SIDE, 3 * FCH), BF16)
    padded[0:SIDE, :] = edge
    padded[SIDE + CELLS : 2 * SIDE + CELLS, :] = edge
    for i, piece in enumerate(with_neighbours(x, SIDE)):
        padded[SIDE : SIDE + CELLS, i * FCH : (i + 1) * FCH] = piece.astype(BF16)
    total = dot(padded[0:CELLS, :], kernel[0])
    total += dot(padded[SIDE : SIDE + CELLS, :], kernel[1])
    total += dot(padded[2 * SIDE : 2 * SIDE + CELLS, :], kernel[2])
    return total


def local_moments(h):
    mean = jnp.sum(h, axis=0, keepdims=True) * (1.0 / h.shape[0])
    away = h - mean
    return mean, jnp.sum(away * away, axis=0, keepdims=True)


def merged(pieces, cells_each):
    count = len(pieces)
    k = pieces[0].shape[0] // 2
    total = functools.reduce(jnp.add, pieces)
    mean = total * (1.0 / count)
    drift = functools.reduce(jnp.add, [jnp.square(piece - mean) for piece in pieces])
    spread = (total[k:] + cells_each * drift[:k]) * (1.0 / (count * cells_each))
    return lanes(mean[:k]), lanes(spread)


def activated(h, mean, spread, gain, shift):
    return jnp.maximum((h - mean) * lax.rsqrt(spread + EPSILON) * gain + shift, 0.0)


def fine_first(tick, *refs):
    if tick == 0:
        place, inflow, pending, mixing, kernels, cpending = refs[:6]
        refs = refs[6:]
    else:
        place, arrived, raised_in, entries, raising, pending, mixing, kernels = refs[:8]
        refs = refs[8:]
    h_ref, pay_ref = refs[:2]
    if tick == 0:
        packed, held, second, mix_ref = refs[2:6]
        x_ref, padded, skip_ref, sems, staged, pack_sems = refs[6:]
    else:
        x_ref, padded, skip_ref, sems, spread_ref, up_ref, up_sems = refs[2:]
        mix_ref = mixing
    segment = place[0]
    kernel = Streamed(kernels.at[0], held, sems.at[pl.ds(0, 3)]) if tick == 0 else kernels
    skip = pltpu.make_async_copy(pending.at[tick], skip_ref, sems.at[3])

    if tick == 0:
        mix = pltpu.make_async_copy(mixing, mix_ref, sems.at[4])
        mix.start()
        x = pltpu.make_async_copy(inflow, x_ref, sems.at[5])
        x.start()
    else:
        up = Streamed(raising, up_ref, up_sems)

        @pl.when(segment == HALF)
        def _():
            up.start()

        @pl.when(segment == 0)
        def _():
            pltpu.make_async_copy(entries.at[tick - 1], x_ref, sems.at[5]).start()

    @pl.when(segment >= HALF)
    def _():
        skip.start()

    if tick == 0:
        kernel.start()
        onward = pltpu.make_async_copy(kernels.at[1], second, pack_sems.at[5])
        onward.start()
        loads = [pltpu.make_async_copy(pending.at[slot], staged.at[slot], pack_sems.at[slot]) for slot in range(4)]
        cloads = [
            pltpu.make_async_copy(
                cpending.at[slot, :, pl.ds(side * FCH, FCH)],
                staged.at[0, pl.ds((2 * slot + side) * CCELLS, CCELLS)],
                pack_sems.at[2 * slot + side],
            )
            for slot in range(2)
            for side in range(2)
        ]
        store = pltpu.make_async_copy(staged, packed, pack_sems.at[4])
        cstore = pltpu.make_async_copy(staged.at[0], packed.at[0], pack_sems.at[4])

        @pl.when(segment < HALF)
        def _():
            for copy in loads:
                copy.start()

        @pl.when(segment >= HALF)
        def _():
            for copy in cloads:
                copy.start()

    if tick == 0:
        x.wait()
    else:

        @pl.when(segment == 0)
        def _():
            pltpu.make_async_copy(entries.at[tick - 1], x_ref, sems.at[5]).wait()

        @pl.when((segment != 0) & (segment != HALF))
        def _():
            x_ref[...] = arrived[...]

        @pl.when(segment == HALF)
        def _():
            for part in range(4):
                raised = dot(raised_in[...], up[part])
                for i in range(CSIDE):
                    start = (2 * i + part // 2) * SIDE + part % 2
                    for p in range(FCH // 128):
                        spread_ref[p, pl.ds(start, CSIDE, stride=2), :] = raised[
                            i * CSIDE : (i + 1) * CSIDE, p * 128 : (p + 1) * 128
                        ]
            for p in range(FCH // 128):
                x_ref[:, p * 128 : (p + 1) * 128] = spread_ref[p].astype(BF16)

    if tick == 0:
        mix.wait()

    @pl.when(segment >= HALF)
    def _():
        skip.wait()
        x_ref[...] = (dot(x_ref[...], mix_ref[...]) + skip_ref[...].astype(F32)).astype(BF16)

    if tick == 0:

        @pl.when(segment < HALF)
        def _():
            for copy in loads:
                copy.wait()
            store.start()

        @pl.when(segment >= HALF)
        def _():
            for copy in cloads:
                copy.wait()
            cstore.start()

    h = fine_convolution(x_ref[...].astype(F32), padded, kernel)
    h_ref[...] = h
    mean, spread = local_moments(h)
    pay = jnp.concatenate(rows_of(mean) + rows_of(spread), axis=0)
    pay_ref[...] = jnp.broadcast_to(pay[None], pay_ref.shape)
    if tick == 0:
        onward.wait()

        @pl.when(segment < HALF)
        def _():
            store.wait()

        @pl.when(segment >= HALF)
        def _():
            cstore.wait()


def coarse_first(tick, *refs):
    place, arrived, pending, mixing, kernels = refs[:5]
    h_ref, mine_ref, other_ref, x_ref, padded, mix_ref, held, sems, skip_ref = refs[5:]
    kernel = Streamed(kernels, held, sems.at[pl.ds(3, 3)])
    if tick < 2:
        skips = [pltpu.make_async_copy(pending.at[tick], skip_ref, sems.at[1])]
    else:
        skips = [
            pltpu.make_async_copy(
                pending.at[0, pl.ds((2 * (tick - 2) + side) * CCELLS, CCELLS)],
                skip_ref.at[:, pl.ds(side * FCH, FCH)],
                sems.at[(1, 6)[side]],
            )
            for side in range(2)
        ]
    segment = place[0]
    mix = pltpu.make_async_copy(mixing, mix_ref, sems.at[0])

    @pl.when(segment < HALF)
    def _():
        mix.start()
        for skip in skips:
            skip.start()

    if tick == 0:
        fetch = pltpu.make_async_copy(arrived, x_ref, sems.at[2])
        fetch.start()
    kernel.start()
    if tick == 0:
        fetch.wait()
    else:
        x_ref[...] = arrived[...]
    @pl.when(segment < HALF)
    def _():
        mix.wait()
        for skip in skips:
            skip.wait()
        x_ref[...] = (dot(x_ref[...], mix_ref[...]) + skip_ref[...].astype(F32)).astype(BF16)

    edge = jnp.zeros((CSIDE, CCH), F32)
    for i, piece in enumerate(with_neighbours(x_ref[...].astype(F32), CSIDE)):
        columns = slice(i * CCH, (i + 1) * CCH)
        padded[0, :, columns] = jnp.concatenate([edge, piece[: CCELLS - CSIDE]], axis=0).astype(BF16)
        padded[1, :, columns] = piece.astype(BF16)
        padded[2, :, columns] = jnp.concatenate([piece[CSIDE:], edge], axis=0).astype(BF16)
    h = dot(padded[0], kernel[0])
    h += dot(padded[1], kernel[1])
    h += dot(padded[2], kernel[2])
    h_ref[...] = h
    mean, spread = local_moments(h)
    mean, spread = rows_of(mean), rows_of(spread)
    first = jnp.concatenate(mean[:2] + spread[:2], axis=0)
    second = jnp.concatenate(mean[2:] + spread[2:], axis=0)
    is_first = place[1] == 0
    mine_ref[...] = jnp.where(is_first, first, second)
    other_ref[...] = jnp.where(is_first, second, first)


def fine_second(gathered, h_ref, gains, shifts, kernel, mine, theirs, out_ref, pay_ref, padded):
    mean, spread = merged([gathered[i] for i in range(N_DP)], float(CELLS))
    x = activated(h_ref[...], mean, spread, gains[0:1], shifts[0:1]).astype(BF16)
    h = fine_convolution(x.astype(F32), padded, kernel)
    out_ref[...] = h
    mean, spread = local_moments(h)
    a, b = mine[...], theirs[...]
    pair_mean = (a[:2] + b[:2]) * 0.5
    pair_spread = a[2:] + b[2:] + jnp.square(a[:2] - b[:2]) * (0.5 * CCELLS)
    pay = jnp.concatenate(rows_of(mean) + rows_of(spread) + [pair_mean, pair_spread], axis=0)
    pay_ref[...] = jnp.broadcast_to(pay[None], pay_ref.shape)


def finish(tick, gathered, h_ref, hc_ref, gains, shifts, cgains, cshifts, fine_ref, coarse_ref):
    mean, spread = merged([gathered[i, 0:4] for i in range(N_DP)], float(CELLS))
    fine_ref[...] = activated(h_ref[...], mean, spread, gains[1:2], shifts[1:2]).astype(BF16)
    mean0, spread0 = merged([gathered[i, 4:8] for i in range(0, N_DP, 2)], 2.0 * CCELLS)
    mean1, spread1 = merged([gathered[i, 4:8] for i in range(1, N_DP, 2)], 2.0 * CCELLS)
    mean = jnp.concatenate([mean0, mean1], axis=1)
    spread = jnp.concatenate([spread0, spread1], axis=1)
    coarse_ref[...] = activated(hc_ref[...], mean, spread, cgains[...], cshifts[...]).astype(BF16)


def coarse_sent(place, fine, coarse, descent, going, fine32, packed, down_ref, sem):
    segment = place[0]

    @pl.when(segment != HALF - 1)
    def _():
        going[...] = coarse[...]

    @pl.when(segment == HALF - 1)
    def _():
        fetch = pltpu.make_async_copy(descent, down_ref, sem)
        fetch.start()
        for p in range(FCH // 128):
            fine32[...] = fine[:, p * 128 : (p + 1) * 128].astype(F32)
            for a in range(2):
                for c in range(2):
                    taken = [fine32[pl.ds((2 * i + a) * SIDE + c, CSIDE, stride=2), :] for i in range(CSIDE)]
                    column = (2 * a + c) * FCH + p * 128
                    packed[:, column : column + 128] = jnp.concatenate(taken, axis=0).astype(BF16)
        fetch.wait()
        going[...] = dot(packed[...], down_ref[...]).astype(BF16)


def keep(tick, *refs):
    place, fine, coarse, mixing, cmixing = refs[:5]
    refs = refs[5:]
    if tick in (0, 2):
        extra, refs = refs[0], refs[1:]
    fstash, cstash, fback, ctarget, term, cterm, mix_ref, cmix_ref, staged, sems = refs[(0, 4, 3, 4)[tick] :]
    segment = place[0]
    copies = [
        pltpu.make_async_copy(fine, fstash.at[tick], sems.at[0]),
        pltpu.make_async_copy(coarse, cstash.at[tick], sems.at[1]),
    ]
    for copy in copies:
        copy.start()
    if tick == 0:
        load = pltpu.make_async_copy(extra.at[4:6], staged.at[0:2], sems.at[2])
        load.start()

    @pl.when(segment < HALF)
    def _():
        fetch = pltpu.make_async_copy(mixing, mix_ref, sems.at[3])
        fetch.start()
        fetch.wait()
        term[...] = dot(fine[...], mix_ref[...]).astype(BF16)
        copy = pltpu.make_async_copy(term, fback.at[2 + tick], sems.at[4])
        copy.start()
        copy.wait()

    @pl.when(segment >= HALF)
    def _():
        fetch = pltpu.make_async_copy(cmixing, cmix_ref, sems.at[3])
        fetch.start()
        if tick == 2:
            received = pltpu.make_async_copy(extra, staged, sems.at[4])
            received.start()
        fetch.wait()
        cterm[...] = dot(coarse[...], cmix_ref[...]).astype(BF16)
        copy = pltpu.make_async_copy(cterm, ctarget.at[tick % 2], sems.at[5])
        copy.start()
        if tick == 2:
            received.wait()
            stored = pltpu.make_async_copy(staged, fback.at[2:6], sems.at[4])
            stored.start()
            stored.wait()
        copy.wait()

    if tick == 0:
        load.wait()
        store = pltpu.make_async_copy(staged.at[0:2], fback.at[0:2], sems.at[2])
        store.start()
        store.wait()
    for copy in copies:
        copy.wait()


def settle(place, received, _, target, sem):
    @pl.when(place[0] < HALF)
    def _():
        copy = pltpu.make_async_copy(received, target, sem)
        copy.start()
        copy.wait()


def kept_after(tick, common, added, kept):
    stashes = [
        (pltpu.HBM, (TICKS, CELLS, FCH)),
        (pltpu.HBM, (TICKS, CCELLS, CCH)),
        (pltpu.HBM, (6, CELLS, FCH)),
        (pltpu.HBM, (2, CCELLS, CCH)),
    ]
    earlier = () if tick == 0 else tuple(kept[:3]) if tick == 2 else tuple(kept)
    start = len(common) + len(added)
    return call(
        functools.partial(keep, tick),
        stashes,
        [SM, VM, VM, ANY, ANY] + [ANY] * (len(added) + len(earlier)),
        (
            pltpu.VMEM((CELLS, FCH), BF16),
            pltpu.VMEM((CCELLS, CCH), BF16),
            pltpu.VMEM((FCH, FCH), BF16),
            pltpu.VMEM((CCH, CCH), BF16),
            pltpu.VMEM((4, CELLS, FCH), BF16),
            pltpu.SemaphoreType.DMA((6,)),
        ),
        40_000_000,
        1_000_000,
        {start + i: i for i in range(len(earlier))},
    )(*common, *added, *earlier)


def tied(*values):
    return lax.optimization_barrier(values)


def on_device(
    fine_inflow,
    coarse_inflow,
    fine_entries,
    fine_pending,
    coarse_pending,
    fine_kernels,
    fine_mixing,
    fine_gains,
    fine_shifts,
    coarse_kernel,
    coarse_mixing,
    coarse_gains,
    coarse_shifts,
    descent_kernel,
    upsample_kernel,
):
    place = jnp.stack([lax.axis_index("segment"), lax.axis_index("dp") % 2]).astype(jnp.int32)
    inflow = fine_inflow.reshape(CELLS, FCH)
    cinflow = coarse_inflow.reshape(CCELLS, CCH)
    entries = fine_entries.reshape(TICKS - 1, CELLS, FCH)
    pending = fine_pending.reshape(6, CELLS, FCH)
    cpending = coarse_pending.reshape(2, CCELLS, CCH)
    kernels = fine_kernels.reshape(2, 3, 3 * FCH, FCH)
    ckernel = coarse_kernel.reshape(3, 3 * CCH, CCH)
    mixing = fine_mixing.reshape(FCH, FCH)
    cmixing = coarse_mixing.reshape(CCH, CCH)
    gains, shifts = fine_gains.reshape(2, FCH), fine_shifts.reshape(2, FCH)
    cgains, cshifts = coarse_gains.reshape(1, CCH), coarse_shifts.reshape(1, CCH)
    descent = descent_kernel.reshape(4 * FCH, CCH)
    upsampling = upsample_kernel.transpose(1, 2, 0, 3).reshape(4, CCH, FCH)

    fine_route = [(0, 1), (1, 2), (2, 3), (4, 5), (5, 6), (6, 7)]
    up_route = [(HALF - 1, HALF)]
    coarse_route = [(p, (p + 1) % (2 * HALF)) for p in range(2 * HALF)]
    to_decoder = [(p, p + HALF) for p in range(HALF)]
    to_encoder = [(p + HALF, p) for p in range(HALF)]
    cores = [(i, i ^ 1) for i in range(N_DP)]

    ftile, ctile = (CELLS, FCH), (CCELLS, CCH)
    fine_bf, coarse_bf = pltpu.VMEM(ftile, BF16), pltpu.VMEM(ctile, BF16)
    padded = pltpu.VMEM((CELLS + 2 * SIDE, 3 * FCH), BF16)
    vmem, hbm = pltpu.VMEM, pltpu.HBM
    kernel_kept = (vmem, (3, 3 * FCH, FCH))
    conv_flops = 2 * CELLS * 9 * FCH * FCH

    arrived = raised = carrived = kept = None
    for tick in range(TICKS):
        sending = tick < TICKS - 1
        if tick == 0:
            sources, specs = (inflow, pending, mixing, kernels, cpending), [SM, ANY, ANY, ANY, ANY, ANY]
            more = (pltpu.VMEM((4, CELLS, FCH), BF16), pltpu.SemaphoreType.DMA((6,)))
        else:
            sources = (arrived, raised, entries, upsampling, pending, near_mixing, kernel_one)
            specs = [SM, VM, VM, ANY, ANY, ANY, VM, VM]
            more = (
                pltpu.VMEM((2, CELLS, 128), F32),
                pltpu.VMEM((4, CCH, FCH), BF16),
                pltpu.SemaphoreType.DMA((4,)),
            )
        h1, pay, *handed = call(
            functools.partial(fine_first, tick),
            [(vmem, ftile, F32), (vmem, (N_DP, 4, 128), F32)] + ([(hbm, (4, CELLS, FCH)), kernel_kept, kernel_kept, (vmem, (FCH, FCH))] if tick == 0 else []),
            specs,
            (fine_bf, padded, fine_bf, pltpu.SemaphoreType.DMA((6,)), *more),
            conv_flops,
            1_000_000,
        )(place, *sources)

        if tick == 0:
            carrived = cinflow
            packed, kernel_one, kernel_two, near_mixing = handed
            pay, later = tied(pay, place)
        else:
            pay, carrived = tied(pay, carrived)
            later = place
        gathered = lax.all_to_all(pay, "dp", 0, 0, tiled=True)
        hc, mine, other = call(
            functools.partial(coarse_first, tick),
            [(vmem, ctile, F32), (vmem, (4, 128), F32), (vmem, (4, 128), F32)],
            [SM, VM if tick else ANY, ANY, ANY, ANY],
            (
                coarse_bf,
                pltpu.VMEM((3, CCELLS, 3 * CCH), BF16),
                pltpu.VMEM((CCH, CCH), BF16),
                pltpu.VMEM((3, 3 * CCH, CCH), BF16),
                pltpu.SemaphoreType.DMA((7,)),
                coarse_bf,
            ),
            2 * CCELLS * 9 * CCH * CCH,
            1_500_000,
        )(later, carrived, cpending if tick < 2 else skips, cmixing, ckernel)
        theirs = lax.ppermute(other, "dp", cores)
        if tick == 2:
            gathered, skips = tied(gathered, skips)
        h2, pay2 = call(
            fine_second,
            [(vmem, ftile, F32), (vmem, (N_DP, 8, 128), F32)],
            [VM] * 7,
            (padded,),
            conv_flops,
            1_000_000,
        )(gathered, h1, gains, shifts, kernel_two, mine, theirs)
        if tick > 0:
            pay2, own, cown = tied(pay2, own, cown)
        if tick == 1:
            pay2, packed = tied(pay2, packed)
        gathered2 = lax.all_to_all(pay2, "dp", 0, 0, tiled=True)
        if tick == 1:
            skips = lax.ppermute(packed, "segment", to_decoder + to_encoder)
        if tick > 0:
            added = ((pending,), (), (skips,))[tick - 1]
            kept = kept_after(tick - 1, (place, own, cown, mixing, cmixing), added, kept)
            gathered2, *kept = tied(gathered2, *kept)
            if tick == 2:
                fresh = lax.ppermute(kept[3], "segment", to_encoder)
        own, cown = call(
            functools.partial(finish, tick),
            [(vmem, ftile), (vmem, ctile)],
            [VM] * 7,
            (),
            1_000_000,
            1_000_000,
        )(gathered2, h2, hc, gains, shifts, cgains, cshifts)
        if sending:
            raised = lax.ppermute(cown, "segment", up_route)
            arrived = lax.ppermute(own, "segment", fine_route)
            (going,) = call(
                coarse_sent,
                [(vmem, ctile)],
                [SM, VM, VM, ANY],
                (
                    pltpu.VMEM((CELLS, 128), F32),
                    pltpu.VMEM((CCELLS, 4 * FCH), BF16),
                    pltpu.VMEM((4 * FCH, CCH), BF16),
                    pltpu.SemaphoreType.DMA,
                ),
                100_000_000,
                1_000_000,
            )(place, own, cown, descent)
            carrived = lax.ppermute(going, "segment", coarse_route)
    fstash, cstash, fback, cback = kept_after(
        TICKS - 1, (place, own, cown, mixing, cmixing), (), kept
    )
    (cback,) = call(
        settle,
        [(hbm, (2, CCELLS, CCH))],
        [SM, VM, ANY],
        (pltpu.SemaphoreType.DMA,),
        0,
        300_000,
        {2: 0},
    )(place, fresh, cback)
    return (
        fstash.reshape(1, TICKS, 1, SIDE, SIDE, FCH),
        cstash.reshape(1, TICKS, 1, CSIDE, CSIDE, CCH),
        fback.reshape(1, 6, 1, SIDE, SIDE, FCH),
        cback.reshape(1, 2, 1, CSIDE, CSIDE, CCH),
    )


def solution(mesh):
    placed = (
        P("segment", "dp", None, None, None),
        P("segment", "dp", None, None, None),
        P(None, "dp", None, None, None),
        P("segment", None, "dp", None, None, None),
        P("segment", None, "dp", None, None, None),
        P("segment", None, None, None, None, None),
        P("segment", None, None),
        P("segment", None, None),
        P("segment", None, None),
        P("segment", None, None, None, None),
        P("segment", None, None),
        P("segment", None),
        P("segment", None),
        P(),
        P(),
    )
    return jax.shard_map(
        on_device,
        mesh=mesh,
        in_specs=placed,
        out_specs=(P("segment", None, "dp", None, None, None),) * 4,
        check_vma=False,
    )
```
